32 devices in a mesh: filt: 2 (over y), chan: 4 (over x, core), tile: 4 (over z).
Axes of the slice: x: 2, y: 2, z: 4, core: 2. Of those that a mesh axis runs over, the one named last changes fastest.
Arguments:
- saved_input: bfloat16 [256, 48, 2048], P('tile', 'filt', 'chan'), may hold values from -1.5 to 1.5
- upstream: bfloat16 [256, 48, 2048], P('tile', None, 'filt'), may hold values from -4 to 4
- kernel: bfloat16 [3, 3, 2048, 2048], P(None, None, 'chan', 'filt'), may hold values from -0.046875 to 0.046875
Outputs:
- input_grad: bfloat16 [256, 48, 2048], P('tile', 'filt', 'chan')
- kernel_grad: float32 [3, 3, 2048, 2048], P(None, None, ('chan', 'tile'), 'filt')
The draws below stay inside these ranges and needn't reach their ends.
All inputs are finite; a program needn't handle non-finite values.
Results may differ from the reference program's by a relative error of at most 0.014.
Values may be sent and summed in bfloat16 or wider, within the bound.
No kernel may reach another device: no remote copies, remote signals or barrier semaphores. Data moves between devices by JAX's collectives and lax.ppermute only.
A program may use at most 192 MiB of HBM per device.

```python
import jax
import jax.numpy as jnp
from jax import lax

CIN = 2048
COUT = 2048
TILE_COLS = 48
HEIGHT = 256
N_FILT = 2


def block_scale(key, shape, cuts, least, high):
    loudness, own = 1.0, jax.random.fold_in(key, 6)
    for dim, parts in cuts:
        draws = jnp.exp(jax.random.uniform(jax.random.fold_in(own, dim), (parts,), jnp.float32, least / len(cuts), high / len(cuts)))
        loudness = loudness * jnp.repeat(draws, shape[dim] // parts).reshape([-1 if axis == dim else 1 for axis in range(len(shape))])
    return loudness


def centred(stream_key, extent, deviation, most, cuts=(), kind=jnp.bfloat16):
    array = jax.random.normal(stream_key, extent, jnp.float32) * deviation
    if len(cuts) > 0:
        array = block_scale(stream_key, extent, cuts, -0.22, 0.18) * array
    return jnp.clip(array, min=-most, max=most).astype(kind)


def setup_inputs(seed: int = 0) -> dict:
    key_of = jax.random.split(jax.random.key(seed), 4)
    saved_input = centred(key_of[0], (HEIGHT, TILE_COLS, CIN), 0.1, 1.5, ((0, 4), (1, 2), (2, 4)))
    upstream = centred(key_of[1], (HEIGHT, TILE_COLS, COUT), 0.25, 4.0, ((0, 4), (2, 2)))
    kernel = centred(key_of[2], (3, 3, CIN, COUT), (9 * CIN) ** -0.5, 0.046875, ((2, 4), (3, 2)))
    return {"saved_input": saved_input, "upstream": upstream, "kernel": kernel}


def shifted_blocks(padded, height, breadth, direction):
    pieces = []
    for step_row in (-1, 0, 1):
        for step_col in (-1, 0, 1):
            top = 1 + direction * step_row
            left = 1 + direction * step_col
            pieces.append(padded[top:top + height, left:left + breadth])
    return jnp.concatenate(pieces, axis=2)


def reference(saved_input, upstream, kernel):
    height, breadth, in_width = saved_input.shape
    out_width = upstream.shape[2]
    block_width = out_width // N_FILT
    active = jnp.maximum(saved_input, jnp.zeros((), jnp.bfloat16))
    padded_grad = jnp.pad(upstream, ((1, 1), (1, 1), (0, 0)))
    stacked_grad = shifted_blocks(padded_grad, height, breadth, -1).reshape(height * breadth, 9, out_width)
    kernel_nine = jnp.transpose(kernel.reshape(9, in_width, out_width), (0, 2, 1))
    active_grad = jnp.zeros((height * breadth, in_width), jnp.float32)
    for block in range(N_FILT):
        low = block * block_width
        grad_piece = stacked_grad[:, :, low:low + block_width].reshape(height * breadth, 9 * block_width)
        kernel_piece = kernel_nine[:, low:low + block_width, :].reshape(9 * block_width, in_width)
        block_grad = jnp.dot(grad_piece, kernel_piece, preferred_element_type=jnp.float32).astype(jnp.bfloat16)
        block_grad = lax.optimization_barrier(block_grad)
        active_grad = active_grad + block_grad.astype(jnp.float32)
    active_grad = active_grad.reshape(height, breadth, in_width)
    input_grad = jnp.where(saved_input > 0, active_grad, jnp.zeros((), jnp.float32)).astype(jnp.bfloat16)
    padded_input = jnp.pad(active, ((1, 1), (1, 1), (0, 0)))
    stacked_input = shifted_blocks(padded_input, height, breadth, 1).reshape(height * breadth, 9 * in_width)
    kernel_grad = jnp.dot(stacked_input.T, upstream.reshape(height * breadth, out_width), preferred_element_type=jnp.float32)
    return input_grad, kernel_grad.reshape(3, 3, in_width, out_width)
```

```python
import jax
import jax.numpy as jnp
from jax import lax
from jax.experimental import pallas as pl
from jax.experimental.pallas import tpu as pltpu
from jax.sharding import PartitionSpec as P

LANES = 128
VMEM = 56 << 20


def largest(total, most):
    return max(n for n in range(1, most + 1) if total % n == 0)


def cost(flops, moved):
    return pl.CostEstimate(flops=flops, bytes_accessed=moved, transcendentals=0)


def params():
    return pltpu.CompilerParams(vmem_limit_bytes=VMEM)


def swap(value, axis, bit):
    count = lax.axis_size(axis)
    return lax.ppermute(value, axis, [(i, i ^ bit) for i in range(count)])


def shifted_active(parts, side):
    height, part, depth = parts[0].shape
    breadth = part * len(parts)
    rows = largest(height, 16)
    span = rows * breadth

    def body(side_ref, *refs):
        *part_refs, out_ref = refs
        read = [ref[...].astype(jnp.float32) for ref in part_refs]
        if len(read) == 2:
            whole = jnp.where(
                side_ref[0] == 0, jnp.concatenate(read, 1), jnp.concatenate(read[::-1], 1)
            )
        else:
            whole = read[0]
        active = jnp.maximum(whole, 0.0).reshape(span, depth).T
        column = lax.broadcasted_iota(jnp.int32, active.shape, 1) % breadth
        before = jnp.where(column == 0, 0.0, pltpu.roll(active, 1, 1))
        after = jnp.where(column == breadth - 1, 0.0, pltpu.roll(active, span - 1, 1))
        out_ref[0] = before.astype(jnp.bfloat16)
        out_ref[1] = active.astype(jnp.bfloat16)
        out_ref[2] = after.astype(jnp.bfloat16)

    return pl.pallas_call(
        body,
        grid_spec=pltpu.PrefetchScalarGridSpec(
            num_scalar_prefetch=1,
            grid=(height // rows,),
            in_specs=[pl.BlockSpec((rows, part, depth), lambda i, s: (i, 0, 0))] * len(parts),
            out_specs=pl.BlockSpec((3, depth, span), lambda i, s: (0, 0, i)),
        ),
        out_shape=jax.ShapeDtypeStruct((3, depth, height * breadth), jnp.bfloat16),
        compiler_params=params(),
        cost_estimate=cost(0, 8 * height * breadth * depth),
        name="shifted_active",
    )(side, *parts)


def kernel_sums(blocks, own_active, pair_active, own_grad, pair_grads, dtype, pair_place=0):
    depth = own_active.shape[1]
    height, breadth, width = pair_grads[0].shape
    height, count = height - 2, len(pair_grads)
    rows = largest(height, 16)
    steps, span, total = height // rows, rows * breadth, width * count

    def body(blocks_ref, own_a, pair_a, *refs):
        own_g, pair_g = refs[:count], refs[count : 2 * count]
        out_ref, sums = refs[2 * count :]
        step = pl.program_id(0)

        def add(active_ref, grad_refs, first_row, fresh):
            active = active_ref[...].reshape(3 * depth, span)
            for r in range(3):
                grads = [
                    ref[pl.ds(first_row + 2 - r, rows)].reshape(span, width) for ref in grad_refs
                ]
                grad = grads[0] if count == 1 else jnp.concatenate(grads, 1)
                product = jnp.dot(active, grad, preferred_element_type=jnp.float32)
                if fresh:
                    sums[r] = product
                else:
                    sums[r] += product

        @pl.when(step == 0)
        def _():
            add(own_a, own_g, 0, True)

        @pl.when((step > 0) & (step < steps))
        def _():
            add(own_a, own_g, step * rows, False)

        @pl.when(step >= steps)
        def _():
            add(pair_a, pair_g, (step - steps) * rows, False)

        @pl.when(step == 2 * steps - 1)
        def _():
            out_ref[...] = sums[...].astype(dtype)

    def own_block(k):
        return pl.BlockSpec((height + 2, breadth, width), lambda i, b: (0, 0, b[k]))

    moved = 2 * (6 * depth + 2 * total) * height * breadth + 9 * depth * total * 4
    return pl.pallas_call(
        body,
        grid_spec=pltpu.PrefetchScalarGridSpec(
            num_scalar_prefetch=1,
            grid=(2 * steps,),
            in_specs=[
                pl.BlockSpec((3, depth, span), lambda i, b: (0, 0, jnp.minimum(i, steps - 1))),
                pl.BlockSpec(
                    (3, depth, span),
                    lambda i, b: (0, 0, jnp.maximum(i - steps, 0) + pair_place * steps),
                ),
                *[own_block(k) for k in range(count)],
                *[pl.BlockSpec((height + 2, breadth, width), lambda i, b: (0, 0, 0))] * count,
            ],
            out_specs=pl.BlockSpec((3, 3 * depth, total), lambda i, b: (0, 0, 0)),
            scratch_shapes=[pltpu.VMEM((3, 3 * depth, total), jnp.float32)],
        ),
        out_shape=jax.ShapeDtypeStruct((3, 3 * depth, total), dtype),
        compiler_params=params(),
        cost_estimate=cost(4 * 9 * depth * total * height * breadth, moved),
        name="kernel_sums",
    )(blocks, own_active, pair_active, *[own_grad] * count, *pair_grads)


def add_block(blocks, near, arrived, out, width, full):
    taps, depth, total = near.shape

    def body(blocks_ref, near_ref, arrived_ref, *refs):
        refs[-1][...] = near_ref[...] + arrived_ref[...].astype(jnp.float32)

    block = (taps, depth, width)
    return pl.pallas_call(
        body,
        grid_spec=pltpu.PrefetchScalarGridSpec(
            num_scalar_prefetch=1,
            grid=(total // width,),
            in_specs=[pl.BlockSpec(block, lambda i, b: (0, 0, i))] * 2
            + [pl.BlockSpec(memory_space=pl.ANY)] * (out is not None),
            out_specs=pl.BlockSpec(block, lambda i, b: (0, 0, b[i])),
        ),
        out_shape=jax.ShapeDtypeStruct((taps, depth, full), jnp.float32),
        input_output_aliases={} if out is None else {3: 0},
        compiler_params=params(),
        cost_estimate=cost(taps * depth * total, 10 * taps * depth * total),
        name="add_block",
    )(blocks, near, arrived, *([] if out is None else [out]))


def block_grad(grad, weights, start, count):
    height, breadth, filters = grad.shape
    depth = weights.shape[1] // 3
    rows = largest(count, 16)
    span = rows * breadth
    lane = min(depth, LANES)

    def body(grad_ref, weights_ref, out_ref, sums):
        first = start + pl.program_id(0) * rows
        for r in range(3):
            moved = grad_ref[pl.ds(first + 2 - r, rows)].reshape(span, filters)
            for s in range(3):
                product = lax.dot_general(
                    moved,
                    weights_ref[r, s * depth : (s + 1) * depth, :],
                    (((1,), (1,)), ((), ())),
                    preferred_element_type=jnp.float32,
                )
                if r == 0:
                    sums[s] = product
                else:
                    sums[s] += product
        column = lax.broadcasted_iota(jnp.int32, (span, lane), 0) % breadth
        for low in range(0, depth, lane):
            before = pltpu.roll(sums[2, :, low : low + lane], 1, 0)
            after = pltpu.roll(sums[0, :, low : low + lane], span - 1, 0)
            value = (
                sums[1, :, low : low + lane]
                + jnp.where(column == 0, 0.0, before)
                + jnp.where(column == breadth - 1, 0.0, after)
            )
            out_ref[:, :, low : low + lane] = value.astype(jnp.bfloat16).reshape(
                rows, breadth, lane
            )

    return pl.pallas_call(
        body,
        grid=(count // rows,),
        in_specs=[
            pl.BlockSpec(
                (height, breadth, filters), lambda i: (0, 0, 0), pipeline_mode=pl.Buffered(1)
            ),
            pl.BlockSpec(weights.shape, lambda i: (0, 0, 0), pipeline_mode=pl.Buffered(1)),
        ],
        out_specs=pl.BlockSpec((rows, breadth, depth), lambda i: (i, 0, 0)),
        scratch_shapes=[pltpu.VMEM((3, span, depth), jnp.float32)],
        out_shape=jax.ShapeDtypeStruct((count, breadth, depth), jnp.bfloat16),
        compiler_params=params(),
        cost_estimate=cost(
            18 * count * breadth * depth * filters, 2 * (grad.size + weights.size)
        ),
        name="block_grad",
    )(grad, weights)


def per_device(saved_input, upstream, kernel):
    height, breadth, filters = upstream.shape
    part = saved_input.shape[1]
    channels = kernel.shape[2]
    tiles, chans, filts = (lax.axis_size(a) for a in ("tile", "chan", "filt"))
    tile, chan, filt = (lax.axis_index(a) for a in ("tile", "chan", "filt"))
    depth = channels // tiles
    side = jnp.reshape(filt, (1,)).astype(jnp.int32)

    up = [(i, i + 1) for i in range(tiles - 1)]
    before = lax.ppermute(upstream[height - 1 :], "tile", up)
    after = lax.ppermute(upstream[:1], "tile", [(j, i) for i, j in up])

    def chunk(bits):
        return lax.dynamic_slice_in_dim(saved_input, (tile ^ bits) * depth, depth, axis=2)

    def columns(value):
        if filts == 2:
            return [value, swap(value, "filt", 1)]
        return [lax.all_gather(value, "filt", axis=1, tiled=True)]

    pair_far = swap(chunk(2), "tile", 1)
    own_far_active = shifted_active(columns(chunk(3)), side)

    def border(low, width):
        return jnp.concatenate(
            [lax.dynamic_slice_in_dim(v, low, width, axis=2) for v in (before, upstream, after)],
            axis=0,
        )

    if chans == 4 and filters % (chans * LANES) == 0:
        share = filters // chans
        width = LANES
        groups = []
        for low in range(0, share, width):
            mine = swap(border(chan * share + low, width), "tile", 1)
            across = swap(mine, "chan", 2)
            groups.append(
                [
                    (0, low, mine),
                    (1, low, swap(mine, "chan", 1)),
                    (2, low, across),
                    (3, low, swap(across, "chan", 1)),
                ]
            )
        groups = [g[:2] for g in groups] + [g[2:] for g in groups]
        pieces = [
            (
                jnp.stack([((chan ^ k) * share + low) // width for k, low, _ in g]).astype(
                    jnp.int32
                ),
                [v for _, _, v in g],
            )
            for g in groups
        ]
    else:
        width = filters
        pieces = [(jnp.zeros((1,), jnp.int32), [swap(border(0, filters), "tile", 1)])]

    pair_far_active = shifted_active(columns(pair_far), side)
    pair_near = swap(chunk(1), "tile", 1)
    near_active = shifted_active(
        columns(jnp.concatenate([chunk(0), pair_near], axis=0)), side
    )

    rimmed = jnp.concatenate([before, upstream, after], axis=0)
    weights = kernel.reshape(3, 3 * channels, filters)

    arrived = []
    for blocks, grads in pieces:
        far = kernel_sums(blocks, own_far_active, pair_far_active, rimmed, grads, jnp.bfloat16)
        arrived.append(swap(far, "tile", 3))

    halves = 2 if height % 2 == 0 else 1
    count = height // halves
    input_grads = []
    for half in range(halves):
        partial = block_grad(rimmed, weights, half * count, count)
        if filts == 2:
            mine = lax.dynamic_slice_in_dim(partial, filt * part, part, axis=1)
            other = lax.dynamic_slice_in_dim(partial, (1 - filt) * part, part, axis=1)
            other = swap(other, "filt", 1)
            summed = mine.astype(jnp.float32) + other.astype(jnp.float32)
        else:
            summed = lax.psum_scatter(
                partial, "filt", scatter_dimension=1, tiled=True
            ).astype(jnp.float32)
        saved = saved_input[half * count : (half + 1) * count]
        input_grads.append(
            jnp.where(saved > 0, summed, jnp.zeros((), jnp.float32)).astype(jnp.bfloat16)
        )
    input_grad = jnp.concatenate(input_grads, axis=0)

    out = None
    for (blocks, grads), result in zip(pieces, arrived):
        near = kernel_sums(
            blocks, near_active, near_active, rimmed, grads, jnp.float32, pair_place=1
        )
        out = add_block(blocks, near, result, out, width, filters)
    return input_grad, out.reshape(3, 3, depth, filters)


def solution(mesh):
    placed = (P("tile", "filt", "chan"), P("tile", None, "filt"), P(None, None, "chan", "filt"))
    return jax.shard_map(
        per_device,
        mesh=mesh,
        in_specs=placed,
        out_specs=(P("tile", "filt", "chan"), P(None, None, ("chan", "tile"), "filt")),
        check_vma=False,
    )
```

```python
import dataclasses
from collections.abc import Callable

import jax
import jax.numpy as jnp
from jax import lax
from jax.experimental import pallas as pl
from jax.experimental.pallas import tpu as pltpu
from jax.sharding import PartitionSpec as P

LANES = 128
VMEM = 62 << 20
ANY = pl.BlockSpec(memory_space=pl.ANY)


def largest(total, most):
    return max(n for n in range(1, most + 1) if total % n == 0)


def cost(flops, moved):
    return pl.CostEstimate(flops=flops * 8, bytes_accessed=moved * 8, transcendentals=0)


def params():
    return pltpu.CompilerParams(vmem_limit_bytes=VMEM)


def swap(value, axis, bit):
    count = lax.axis_size(axis)
    return lax.ppermute(value, axis, [(i, i ^ bit) for i in range(count)])


class Stream:
    def __init__(self, groups, ahead):
        self.groups, self.ahead, self.begun = groups, ahead, 0
        self.begin(ahead)

    def begin(self, upto):
        while self.begun < min(upto, len(self.groups)):
            for copy in self.groups[self.begun]:
                copy.start()
            self.begun += 1

    def wait(self, k):
        for copy in self.groups[k]:
            copy.wait()
        self.begin(k + 1 + self.ahead)


@dataclasses.dataclass
class Part:
    body: Callable
    operands: list
    outs: list
    scratch: list
    work: tuple


def run(name, parts, after):
    ins = [len(p.operands) for p in parts]
    outs = [len(p.outs) for p in parts]
    scratch = [len(p.scratch) for p in parts]

    def split(refs, counts):
        lists, at = [], 0
        for n in counts:
            lists.append(refs[at : at + n])
            at += n
        return lists

    def body(*refs):
        first = sum(ins) + len(after)
        inputs = split(refs[: sum(ins)], ins)
        results = split(refs[first : first + sum(outs)], outs)
        held = split(refs[first + sum(outs) :], scratch)
        steps = [p.body(i, o, h) for p, i, o, h in zip(parts, inputs, results, held)]
        for step in steps:
            next(step)
        for step in steps:
            for _ in step:
                pass

    flat = pl.pallas_call(
        body,
        in_specs=[ANY] * (sum(ins) + len(after)),
        out_specs=[spec for p in parts for _, spec in p.outs],
        scratch_shapes=[x for p in parts for x in p.scratch],
        out_shape=[shape for p in parts for shape, _ in p.outs],
        compiler_params=params(),
        cost_estimate=cost(sum(p.work[0] for p in parts), sum(p.work[1] for p in parts)),
        name=name,
    )(*[x for p in parts for x in p.operands], *after)
    return split(flat, outs)


def shifted_active(parts, after):
    height, part, depth = parts[0].shape
    breadth = part * len(parts)
    rows = largest(height, 32)
    span = rows * breadth

    def body(*refs):
        part_refs, out_ref = refs[: len(parts)], refs[-1]
        read = [jnp.maximum(ref[...].astype(jnp.float32), 0.0) for ref in part_refs]
        whole = read[0]
        if len(read) == 2:
            whole = jnp.where(
                lax.axis_index("filt") == 0,
                jnp.concatenate(read, 1),
                jnp.concatenate(read[::-1], 1),
            )
        active = whole.reshape(span, depth).T
        column = lax.broadcasted_iota(jnp.int32, (1, span), 1) % breadth
        before = jnp.where(column == 0, 0.0, pltpu.roll(active, 1, 1))
        behind = jnp.where(column == breadth - 1, 0.0, pltpu.roll(active, span - 1, 1))
        out_ref[0] = before.astype(jnp.bfloat16)
        out_ref[1] = active.astype(jnp.bfloat16)
        out_ref[2] = behind.astype(jnp.bfloat16)

    return pl.pallas_call(
        body,
        grid=(height // rows,),
        in_specs=[pl.BlockSpec((rows, part, depth), lambda i: (i, 0, 0))] * len(parts)
        + [ANY] * len(after),
        out_specs=pl.BlockSpec((3, depth, span), lambda i: (0, 0, i)),
        out_shape=jax.ShapeDtypeStruct((3, depth, height * breadth), jnp.bfloat16),
        compiler_params=params(),
        cost_estimate=cost(0, 8 * height * breadth * depth),
        name="shifted_active",
    )(*parts, *after)


def column_slice(index, width):
    start = index * width
    return pl.ds(pl.multiple_of(start, width) if width % LANES == 0 else start, width)


def sums_part(blocks, order, own, pair, own_grad, rims, arrived=(), full=None):
    (own_active, own_at), (pair_active, pair_at) = own, pair
    depth = own_active.shape[1]
    parts, count = len(blocks[0][1]), len(blocks)
    share, breadth, width = blocks[0][1][0].shape
    height = share * parts
    total = width * count
    cuts = [[0, height // 4, height], [0, height]] if height % 4 == 0 else [[0, height]] * 2
    waits = sum(len(c) - 1 for c in cuts)
    dtype = jnp.bfloat16 if full is None else jnp.float32
    outs = count if full is None else 1

    def body(inputs, out_refs, scratch):
        own_a, pair_a, own_g, rims_ref, *refs = inputs
        pieces = [refs[parts * b : parts * (b + 1)] for b in range(count)]
        arrived_refs = refs[parts * count :]
        actives, grads, sums, came, a_sem, g_sem, r_sem, p_sem, c_sem, o_sem = scratch
        columns = [column_slice(place(), width) for place, _ in blocks]
        held = [pl.ds(b * width, width) for b in range(count)]

        def load(t, k, low, high):
            group = []
            if low == 0:
                for b in range(count):
                    for e in range(2):
                        group.append(
                            pltpu.make_async_copy(
                                rims_ref.at[pl.ds(2 * t + e, 1), :, columns[b]],
                                grads.at[t, pl.ds(e * (height + 1), 1), :, held[b]],
                                r_sem.at[t, b, e],
                            )
                        )
            if t == 0:
                first, last = low + (low > 0), min(high + 1, height)
                for b in range(count):
                    group.append(
                        pltpu.make_async_copy(
                            own_g.at[pl.ds(first, last - first), :, columns[b]],
                            grads.at[0, pl.ds(first + 1, last - first), :, held[b]],
                            g_sem.at[k, b],
                        )
                    )
            elif low == 0:
                for b in range(count):
                    for k_piece in range(parts):
                        group.append(
                            pltpu.make_async_copy(
                                pieces[b][k_piece],
                                grads.at[1, pl.ds(order(k_piece) * share + 1, share), :, held[b]],
                                p_sem.at[b, k_piece],
                            )
                        )
            ref, at = ((own_a, own_at), (pair_a, pair_at))[t]
            group.append(
                pltpu.make_async_copy(
                    ref.at[:, :, pl.ds((at * height + low) * breadth, (high - low) * breadth)],
                    actives.at[t, :, :, pl.ds(low * breadth, (high - low) * breadth)],
                    a_sem.at[t, k],
                )
            )
            return group

        spans = [
            (t, k, cuts[t][k], cuts[t][k + 1]) for t in range(2) for k in range(len(cuts[t]) - 1)
        ]
        groups = [load(*span) for span in spans]
        groups[-1] += [
            pltpu.make_async_copy(ref, came.at[:, :, held[b]], c_sem.at[b])
            for b, ref in enumerate(arrived_refs)
        ]
        stream = Stream(groups, 2)
        yield
        for n, (t, k, low, high) in enumerate(spans):
            stream.wait(n)
            active = actives[t, :, :, low * breadth : high * breadth]
            active = active.reshape(3 * depth, (high - low) * breadth)
            for r in range(3):
                grad = grads[t, low + 2 - r : high + 2 - r].reshape((high - low) * breadth, total)
                product = jnp.dot(active, grad, preferred_element_type=jnp.float32)
                if n > 0:
                    product += sums[r]
                if n == waits - 1 and arrived:
                    known = width * len(arrived)
                    extra = came[r, :, :known].astype(jnp.float32)
                    sums[r, :, :known] = product[:, :known] + extra
                    sums[r, :, known:] = product[:, known:]
                elif n == waits - 1 and full is None:
                    for b in range(count):
                        out_refs[b][r] = product[:, b * width : (b + 1) * width].astype(dtype)
                else:
                    sums[r] = product
        if full is not None:
            stores = [
                pltpu.make_async_copy(
                    sums.at[:, :, held[b]], out_refs[0].at[:, :, columns[b]], o_sem.at[b]
                )
                for b in range(count)
            ]
            for c in stores:
                c.start()
            for c in stores:
                c.wait()

    moved = 2 * (6 * depth + 2 * total) * height * breadth + 9 * depth * total * 4
    operands = [own_active, pair_active, own_grad, rims]
    operands += [piece for _, grads in blocks for piece in grads] + list(arrived)
    shape = jax.ShapeDtypeStruct((3, 3 * depth, full or width), dtype)
    return Part(
        body,
        operands,
        [(shape, pl.BlockSpec(memory_space=pltpu.VMEM) if full is None else ANY)] * outs,
        [
            pltpu.VMEM((2, 3, depth, height * breadth), jnp.bfloat16),
            pltpu.VMEM((2, height + 2, breadth, total), jnp.bfloat16),
            pltpu.VMEM((3, 3 * depth, total), jnp.float32),
            pltpu.VMEM((3, 3 * depth, total if arrived else LANES), jnp.bfloat16),
            pltpu.SemaphoreType.DMA((2, waits)),
            pltpu.SemaphoreType.DMA((waits, count)),
            pltpu.SemaphoreType.DMA((2, count, 2)),
            pltpu.SemaphoreType.DMA((count, parts)),
            pltpu.SemaphoreType.DMA((count,)),
            pltpu.SemaphoreType.DMA((count,)),
        ],
        (4 * 9 * depth * total * height * breadth, moved),
    )


def add_blocks(places, arrived, out, after):
    taps, depth, width = arrived[0].shape
    count = len(arrived)

    def body(*refs):
        arrived_refs = refs[:count]
        out_ref, came, held, sems = refs[-4:]
        steps = [(b, k) for b in range(count) for k in range(taps)]
        columns = [column_slice(place(), width) for place in places]

        def there(b, k):
            return out_ref.at[k, :, columns[b]]

        loads = [
            (
                pltpu.make_async_copy(arrived_refs[b].at[k], came.at[b, k], sems.at[0, b, k]),
                pltpu.make_async_copy(there(b, k), held.at[b, k], sems.at[1, b, k]),
            )
            for b, k in steps
        ]
        stores = [
            pltpu.make_async_copy(held.at[b, k], there(b, k), sems.at[2, b, k]) for b, k in steps
        ]
        for pair in loads:
            for c in pair:
                c.start()
        for n, (b, k) in enumerate(steps):
            for c in loads[n]:
                c.wait()
            held[b, k] += came[b, k].astype(jnp.float32)
            stores[n].start()
        for c in stores:
            c.wait()

    return pl.pallas_call(
        body,
        in_specs=[ANY] * (count + 1 + len(after)),
        out_specs=ANY,
        scratch_shapes=[
            pltpu.VMEM((count, taps, depth, width), jnp.bfloat16),
            pltpu.VMEM((count, taps, depth, width), jnp.float32),
            pltpu.SemaphoreType.DMA((3, count, taps)),
        ],
        out_shape=jax.ShapeDtypeStruct(out.shape, jnp.float32),
        input_output_aliases={count: 0},
        compiler_params=params(),
        cost_estimate=cost(count * taps * depth * width, 10 * count * taps * depth * width),
        name="add_blocks",
    )(*arrived, out, *after)


def cut_share(grad, block, share, width, after):
    breadth = grad.shape[1]

    def body(grad_ref, *refs):
        out_ref, sem = refs[-2:]
        chan = lax.axis_index("chan")
        load = pltpu.make_async_copy(
            grad_ref.at[
                pl.ds(chan % 2 * share, share), :, column_slice(chan // 2 * 2 + block, width)
            ],
            out_ref,
            sem,
        )
        load.start()
        load.wait()

    return pl.pallas_call(
        body,
        in_specs=[ANY] * (1 + len(after)),
        out_specs=pl.BlockSpec(memory_space=pltpu.VMEM),
        scratch_shapes=[pltpu.SemaphoreType.DMA],
        out_shape=jax.ShapeDtypeStruct((share, breadth, width), grad.dtype),
        compiler_params=params(),
        cost_estimate=cost(0, 4 * share * breadth * width),
        name="cut_share",
    )(grad, *after)


def block_part(grad, rims, weights, tops, unit):
    height, breadth, filters = grad.shape
    depth = weights.shape[1] // 3
    span, count = unit * breadth, len(tops)
    lane = min(depth, LANES)

    def body(inputs, out_refs, scratch):
        grad_any, rims_any, weights_any = inputs
        (out_ref,) = out_refs
        grads, taps, sums, results, g_sem, r_sem, w_sem, o_sem = scratch

        def rows_of(n):
            top = tops[n]
            low, high = max(top - 1, 0), min(top + unit + 1, height)
            copies = [
                pltpu.make_async_copy(
                    grad_any.at[pl.ds(low, high - low)],
                    grads.at[n, pl.ds(low - top + 1, high - low)],
                    g_sem.at[n],
                )
            ]
            for e, edge in enumerate((low == top, high == top + unit)):
                if edge:
                    copies.append(
                        pltpu.make_async_copy(
                            rims_any.at[pl.ds(e, 1)],
                            grads.at[n, pl.ds(e * (unit + 1), 1)],
                            r_sem.at[n, e],
                        )
                    )
            return copies

        loads = [
            pltpu.make_async_copy(
                weights_any.at[r, pl.ds(s * depth, depth)],
                taps.at[r, pl.ds(s * depth, depth)],
                w_sem.at[r, s],
            )
            for r in range(3)
            for s in range(3)
        ]
        groups = [rows_of(0) + loads[:1], loads[1:3], loads[3:6], loads[6:]]
        groups += [rows_of(n) for n in range(1, count)]
        stream = Stream(groups, 2)
        yield
        waits = {0: 0, 1: 1, 3: 2, 6: 3}
        column = lax.broadcasted_iota(jnp.int32, (unit, breadth, lane), 1).reshape(span, lane)
        stores = []
        for n, top in enumerate(tops):
            if n > 0:
                stream.wait(3 + n)
            for r in range(3):
                for s in range(3):
                    if n == 0 and 3 * r + s in waits:
                        stream.wait(waits[3 * r + s])
                    moved = grads[n, 2 - r : 2 - r + unit].reshape(span, filters)
                    product = lax.dot_general(
                        moved,
                        taps[r, s * depth : (s + 1) * depth, :],
                        (((1,), (1,)), ((), ())),
                        preferred_element_type=jnp.float32,
                    )
                    if r == 0:
                        sums[s] = product
                    else:
                        sums[s] += product
            for low in range(0, depth, lane):
                before = pltpu.roll(sums[2, :, low : low + lane], 1, 0)
                behind = pltpu.roll(sums[0, :, low : low + lane], span - 1, 0)
                value = (
                    sums[1, :, low : low + lane]
                    + jnp.where(column == 0, 0.0, before)
                    + jnp.where(column == breadth - 1, 0.0, behind)
                )
                results[n, :, :, low : low + lane] = value.astype(jnp.bfloat16).reshape(
                    unit, breadth, lane
                )
            stores.append(
                pltpu.make_async_copy(results.at[n], out_ref.at[pl.ds(n * unit, unit)], o_sem.at[n])
            )
            stores[-1].start()
        for c in stores:
            c.wait()

    shape = jax.ShapeDtypeStruct((count * unit, breadth, depth), jnp.bfloat16)
    return Part(
        body,
        [grad, rims, weights],
        [(shape, ANY)],
        [
            pltpu.VMEM((count, unit + 2, breadth, filters), jnp.bfloat16),
            pltpu.VMEM(weights.shape, jnp.bfloat16),
            pltpu.VMEM((3, span, depth), jnp.float32),
            pltpu.VMEM((count, unit, breadth, depth), jnp.bfloat16),
            pltpu.SemaphoreType.DMA((count,)),
            pltpu.SemaphoreType.DMA((count, 2)),
            pltpu.SemaphoreType.DMA((3, 3)),
            pltpu.SemaphoreType.DMA((count,)),
        ],
        (18 * count * unit * breadth * depth * filters, 2 * weights.size),
    )


def per_device(saved_input, upstream, kernel):
    height, breadth, filters = upstream.shape
    part = saved_input.shape[1]
    channels = kernel.shape[2]
    tiles, chans, filts = (lax.axis_size(a) for a in ("tile", "chan", "filt"))
    tile, filt = (lax.axis_index(a) for a in ("tile", "filt"))
    depth = channels // tiles

    def chunk(bits, saved=saved_input):
        return lax.dynamic_slice_in_dim(saved, (tile ^ bits) * depth, depth, axis=2)

    def columns(value):
        if filts == 2:
            return [value, swap(value, "filt", 1)]
        return [lax.all_gather(value, "filt", axis=1, tiled=True)]

    sent_far = chunk(2)
    pair_far = swap(sent_far, "tile", 1)
    own_far = columns(chunk(3))

    even = tile % 2 == 0
    first, last = upstream[:1], upstream[height - 1 :]
    up = [(i, i + 1) for i in range(tiles - 1)]
    inward, outward = jnp.where(even, last, first), jnp.where(even, first, last)
    above = lax.ppermute(last, "tile", up)
    below = lax.ppermute(first, "tile", [(j, i) for i, j in up])
    across = lax.ppermute(outward, "tile", [(1, 3), (2, 0)])
    rims = jnp.concatenate(
        [above, below, jnp.where(even, inward, across), jnp.where(even, across, inward)], axis=0
    )

    weights = kernel.reshape(3, 3 * channels, filters)
    unit = largest(height, 16)
    tops = list(range(0, height, unit))
    halves = [h for h in (tops[: len(tops) // 2], tops[len(tops) // 2 :]) if h]
    partials = []

    def next_rows(after):
        part_ = block_part(upstream, rims, weights, halves[len(partials)], unit)
        ((partial,),) = run("block_grad", [part_], after)
        partials.append(partial)
        return [partial]

    if chans == 4 and filters % (4 * LANES) == 0 and height % 2 == 0:
        share, width = height // 2, filters // 4
        near_cut = cut_share(upstream, 0, share, width, [sent_far])
        far_cut = cut_share(upstream, 1, share, width, [rims, near_cut])
        own_far = shifted_active(own_far, [far_cut, pair_far])
        fetched = [swap(near_cut, "tile", 1), swap(far_cut, "tile", 1)]
        fetched[0], _ = lax.optimization_barrier((fetched[0], own_far))
        crossed = [swap(v, "chan", 2) for v in fetched]
        pieces = [[v, swap(v, "chan", 1)] for v in fetched]

        def place_of(j):
            return lambda: (lax.axis_index("chan") // 2 ^ (j // 2)) * 2 + j % 2

        def order(k):
            return lax.axis_index("chan") % 2 ^ k

        groups = [[0], [1], [2, 3]]
    else:
        own_far = shifted_active(own_far, [])
        crossed, pieces = [], [[swap(upstream, "tile", 1)]]

        def place_of(j):
            return lambda: 0

        def order(k):
            return 0

        groups = [[0]]
    chain = [own_far]
    pair_far = shifted_active(columns(pair_far), chain)
    chain = [pair_far]
    arrived = []
    saved, _ = lax.optimization_barrier((saved_input, pair_far))
    pair_near = swap(chunk(1, saved), "tile", 1)
    for n, group in enumerate(groups):
        if n == 2:
            pieces += [[v, swap(v, "chan", 1)] for v in crossed]
        blocks = [(place_of(j), v) for j, v in enumerate(pieces)]
        sums = sums_part(
            [blocks[j] for j in group], order, (own_far, 0), (pair_far, 0), upstream, rims
        )
        (far,) = run("kernel_sums", [sums], chain)
        chain = [far[-1]]
        arrived += [swap(v, "tile", 3) for v in far]
        if n == 0:
            pair_near, _ = lax.optimization_barrier((pair_near, far[0]))
            near = columns(jnp.concatenate([chunk(0), pair_near], axis=0))
            chain = next_rows(chain)
    partials[0], _ = lax.optimization_barrier((partials[0], far[-1]))
    while len(partials) < len(halves):
        chain = next_rows(chain)
    near = shifted_active(near, chain)
    last = sums_part(blocks, order, (near, 0), (near, 1), upstream, rims, arrived[:-1], filters)
    ((out,),) = run("kernel_sums", [last], [near])
    summed = []
    for partial in partials:
        if filts == 2:
            mine = lax.dynamic_slice_in_dim(partial, filt * part, part, axis=1)
            other = lax.dynamic_slice_in_dim(partial, (1 - filt) * part, part, axis=1)
            total = mine.astype(jnp.float32) + swap(other, "filt", 1).astype(jnp.float32)
        else:
            total = lax.psum_scatter(partial, "filt", scatter_dimension=1, tiled=True).astype(
                jnp.float32
            )
        summed.append(total)
    masked = jnp.where(saved_input > 0, jnp.concatenate(summed, 0), jnp.zeros((), jnp.float32))
    input_grad = masked.astype(jnp.bfloat16)
    out = add_blocks([blocks[-1][0]], arrived[-1:], out, [input_grad])
    return input_grad, out.reshape(3, 3, depth, filters)


def solution(mesh):
    placed = (P("tile", "filt", "chan"), P("tile", None, "filt"), P(None, None, "chan", "filt"))
    return jax.shard_map(
        per_device,
        mesh=mesh,
        in_specs=placed,
        out_specs=(P("tile", "filt", "chan"), P(None, None, ("chan", "tile"), "filt")),
        check_vma=False,
    )
```

```python
import dataclasses
from collections.abc import Callable

import jax
import jax.numpy as jnp
from jax import lax
from jax.experimental import pallas as pl
from jax.experimental.pallas import tpu as pltpu
from jax.sharding import PartitionSpec as P

LANES = 128
VMEM = 62 << 20
ANY = pl.BlockSpec(memory_space=pl.ANY)


def largest(total, most):
    return max(n for n in range(1, most + 1) if total % n == 0)


def cost(flops, moved):
    return pl.CostEstimate(flops=flops * 8, bytes_accessed=moved * 8, transcendentals=0)


def params():
    return pltpu.CompilerParams(vmem_limit_bytes=VMEM)


def swap(value, axis, bit):
    count = lax.axis_size(axis)
    return lax.ppermute(value, axis, [(i, i ^ bit) for i in range(count)])


class Stream:
    def __init__(self, groups, ahead):
        self.groups, self.ahead, self.begun = groups, ahead, 0
        self.begin(ahead)

    def begin(self, upto):
        while self.begun < min(upto, len(self.groups)):
            for copy in self.groups[self.begun]:
                copy.start()
            self.begun += 1

    def wait(self, k):
        for copy in self.groups[k]:
            copy.wait()
        self.begin(k + 1 + self.ahead)


@dataclasses.dataclass
class Part:
    body: Callable
    operands: list
    outs: list
    scratch: list
    work: tuple


def run(name, parts, after):
    ins = [len(p.operands) for p in parts]
    outs = [len(p.outs) for p in parts]
    scratch = [len(p.scratch) for p in parts]

    def split(refs, counts):
        lists, at = [], 0
        for n in counts:
            lists.append(refs[at : at + n])
            at += n
        return lists

    def body(*refs):
        first = sum(ins) + len(after)
        inputs = split(refs[: sum(ins)], ins)
        results = split(refs[first : first + sum(outs)], outs)
        held = split(refs[first + sum(outs) :], scratch)
        steps = [p.body(i, o, h) for p, i, o, h in zip(parts, inputs, results, held)]
        for step in steps:
            next(step)
        for step in steps:
            for _ in step:
                pass

    flat = pl.pallas_call(
        body,
        in_specs=[ANY] * (sum(ins) + len(after)),
        out_specs=[spec for p in parts for _, spec in p.outs],
        scratch_shapes=[x for p in parts for x in p.scratch],
        out_shape=[shape for p in parts for shape, _ in p.outs],
        compiler_params=params(),
        cost_estimate=cost(sum(p.work[0] for p in parts), sum(p.work[1] for p in parts)),
        name=name,
    )(*[x for p in parts for x in p.operands], *after)
    return split(flat, outs)


def shifted_active(parts, after):
    height, part, depth = parts[0].shape
    breadth = part * len(parts)
    rows = largest(height, 32)
    span = rows * breadth

    def body(*refs):
        part_refs, out_ref = refs[: len(parts)], refs[-1]
        read = [jnp.maximum(ref[...].astype(jnp.float32), 0.0) for ref in part_refs]
        whole = read[0]
        if len(read) == 2:
            whole = jnp.where(
                lax.axis_index("filt") == 0,
                jnp.concatenate(read, 1),
                jnp.concatenate(read[::-1], 1),
            )
        active = whole.reshape(span, depth).T
        column = lax.broadcasted_iota(jnp.int32, (1, span), 1) % breadth
        before = jnp.where(column == 0, 0.0, pltpu.roll(active, 1, 1))
        behind = jnp.where(column == breadth - 1, 0.0, pltpu.roll(active, span - 1, 1))
        out_ref[0] = before.astype(jnp.bfloat16)
        out_ref[1] = active.astype(jnp.bfloat16)
        out_ref[2] = behind.astype(jnp.bfloat16)

    return pl.pallas_call(
        body,
        grid=(height // rows,),
        in_specs=[pl.BlockSpec((rows, part, depth), lambda i: (i, 0, 0))] * len(parts)
        + [ANY] * len(after),
        out_specs=pl.BlockSpec((3, depth, span), lambda i: (0, 0, i)),
        out_shape=jax.ShapeDtypeStruct((3, depth, height * breadth), jnp.bfloat16),
        compiler_params=params(),
        cost_estimate=cost(0, 8 * height * breadth * depth),
        name="shifted_active",
    )(*parts, *after)


def column_slice(index, width):
    start = index * width
    return pl.ds(pl.multiple_of(start, width) if width % LANES == 0 else start, width)


def sums_part(blocks, order, own, pair, own_grad, rims, arrived=(), full=None):
    (own_active, own_at), (pair_active, pair_at) = own, pair
    depth = own_active.shape[1]
    parts, count = len(blocks[0][1]), len(blocks)
    share, breadth, width = blocks[0][1][0].shape
    height = share * parts
    total = width * count
    cuts = [[0, height // 4, height], [0, height]] if height % 4 == 0 else [[0, height]] * 2
    waits = sum(len(c) - 1 for c in cuts)
    dtype = jnp.bfloat16 if full is None else jnp.float32
    outs = count if full is None else 1

    def body(inputs, out_refs, scratch):
        own_a, pair_a, own_g, rims_ref, *refs = inputs
        pieces = [refs[parts * b : parts * (b + 1)] for b in range(count)]
        arrived_refs = refs[parts * count :]
        actives, grads, sums, came, a_sem, g_sem, r_sem, p_sem, c_sem, o_sem = scratch
        columns = [column_slice(place(), width) for place, _ in blocks]
        held = [pl.ds(b * width, width) for b in range(count)]

        def load(t, k, low, high):
            group = []
            if low == 0:
                for b in range(count):
                    for e in range(2):
                        group.append(
                            pltpu.make_async_copy(
                                rims_ref.at[pl.ds(2 * t + e, 1), :, columns[b]],
                                grads.at[t, pl.ds(e * (height + 1), 1), :, held[b]],
                                r_sem.at[t, b, e],
                            )
                        )
            if t == 0:
                first, last = low + (low > 0), min(high + 1, height)
                for b in range(count):
                    group.append(
                        pltpu.make_async_copy(
                            own_g.at[pl.ds(first, last - first), :, columns[b]],
                            grads.at[0, pl.ds(first + 1, last - first), :, held[b]],
                            g_sem.at[k, b],
                        )
                    )
            elif low == 0:
                for b in range(count):
                    for k_piece in range(parts):
                        group.append(
                            pltpu.make_async_copy(
                                pieces[b][k_piece],
                                grads.at[1, pl.ds(order(k_piece) * share + 1, share), :, held[b]],
                                p_sem.at[b, k_piece],
                            )
                        )
            ref, at = ((own_a, own_at), (pair_a, pair_at))[t]
            group.append(
                pltpu.make_async_copy(
                    ref.at[:, :, pl.ds((at * height + low) * breadth, (high - low) * breadth)],
                    actives.at[t, :, :, pl.ds(low * breadth, (high - low) * breadth)],
                    a_sem.at[t, k],
                )
            )
            return group

        spans = [
            (t, k, cuts[t][k], cuts[t][k + 1]) for t in range(2) for k in range(len(cuts[t]) - 1)
        ]
        groups = [load(*span) for span in spans]
        groups[-1] += [
            pltpu.make_async_copy(ref, came.at[:, :, held[b]], c_sem.at[b])
            for b, ref in enumerate(arrived_refs)
        ]
        stream = Stream(groups, 2)
        yield
        for n, (t, k, low, high) in enumerate(spans):
            stream.wait(n)
            active = actives[t, :, :, low * breadth : high * breadth]
            active = active.reshape(3 * depth, (high - low) * breadth)
            for r in range(3):
                grad = grads[t, low + 2 - r : high + 2 - r].reshape((high - low) * breadth, total)
                product = jnp.dot(active, grad, preferred_element_type=jnp.float32)
                if n > 0:
                    product += sums[r]
                if n == waits - 1 and arrived:
                    known = width * len(arrived)
                    extra = came[r, :, :known].astype(jnp.float32)
                    sums[r, :, :known] = product[:, :known] + extra
                    sums[r, :, known:] = product[:, known:]
                elif n == waits - 1 and full is None:
                    for b in range(count):
                        out_refs[b][r] = product[:, b * width : (b + 1) * width].astype(dtype)
                else:
                    sums[r] = product
        if full is not None:
            stores = [
                pltpu.make_async_copy(
                    sums.at[:, :, held[b]], out_refs[0].at[:, :, columns[b]], o_sem.at[b]
                )
                for b in range(count)
            ]
            for c in stores:
                c.start()
            for c in stores:
                c.wait()

    moved = 2 * (6 * depth + 2 * total) * height * breadth + 9 * depth * total * 4
    operands = [own_active, pair_active, own_grad, rims]
    operands += [piece for _, grads in blocks for piece in grads] + list(arrived)
    shape = jax.ShapeDtypeStruct((3, 3 * depth, full or width), dtype)
    return Part(
        body,
        operands,
        [(shape, pl.BlockSpec(memory_space=pltpu.VMEM) if full is None else ANY)] * outs,
        [
            pltpu.VMEM((2, 3, depth, height * breadth), jnp.bfloat16),
            pltpu.VMEM((2, height + 2, breadth, total), jnp.bfloat16),
            pltpu.VMEM((3, 3 * depth, total), jnp.float32),
            pltpu.VMEM((3, 3 * depth, total if arrived else LANES), jnp.bfloat16),
            pltpu.SemaphoreType.DMA((2, waits)),
            pltpu.SemaphoreType.DMA((waits, count)),
            pltpu.SemaphoreType.DMA((2, count, 2)),
            pltpu.SemaphoreType.DMA((count, parts)),
            pltpu.SemaphoreType.DMA((count,)),
            pltpu.SemaphoreType.DMA((count,)),
        ],
        (4 * 9 * depth * total * height * breadth, moved),
    )


def add_blocks(places, arrived, out, after):
    taps, depth, width = arrived[0].shape
    count = len(arrived)

    def body(*refs):
        arrived_refs = refs[:count]
        out_ref, came, held, sems = refs[-4:]
        steps = [(b, k) for b in range(count) for k in range(taps)]
        columns = [column_slice(place(), width) for place in places]

        def there(b, k):
            return out_ref.at[k, :, columns[b]]

        loads = [
            (
                pltpu.make_async_copy(arrived_refs[b].at[k], came.at[b, k], sems.at[0, b, k]),
                pltpu.make_async_copy(there(b, k), held.at[b, k], sems.at[1, b, k]),
            )
            for b, k in steps
        ]
        stores = [
            pltpu.make_async_copy(held.at[b, k], there(b, k), sems.at[2, b, k]) for b, k in steps
        ]
        for pair in loads:
            for c in pair:
                c.start()
        for n, (b, k) in enumerate(steps):
            for c in loads[n]:
                c.wait()
            held[b, k] += came[b, k].astype(jnp.float32)
            stores[n].start()
        for c in stores:
            c.wait()

    return pl.pallas_call(
        body,
        in_specs=[ANY] * (count + 1 + len(after)),
        out_specs=ANY,
        scratch_shapes=[
            pltpu.VMEM((count, taps, depth, width), jnp.bfloat16),
            pltpu.VMEM((count, taps, depth, width), jnp.float32),
            pltpu.SemaphoreType.DMA((3, count, taps)),
        ],
        out_shape=jax.ShapeDtypeStruct(out.shape, jnp.float32),
        input_output_aliases={count: 0},
        compiler_params=params(),
        cost_estimate=cost(count * taps * depth * width, 10 * count * taps * depth * width),
        name="add_blocks",
    )(*arrived, out, *after)


def cut_share(grad, block, share, width, after):
    breadth = grad.shape[1]

    def body(grad_ref, *refs):
        out_ref, sem = refs[-2:]
        chan = lax.axis_index("chan")
        load = pltpu.make_async_copy(
            grad_ref.at[
                pl.ds(chan % 2 * share, share), :, column_slice(chan // 2 * 2 + block, width)
            ],
            out_ref,
            sem,
        )
        load.start()
        load.wait()

    return pl.pallas_call(
        body,
        in_specs=[ANY] * (1 + len(after)),
        out_specs=pl.BlockSpec(memory_space=pltpu.VMEM),
        scratch_shapes=[pltpu.SemaphoreType.DMA],
        out_shape=jax.ShapeDtypeStruct((share, breadth, width), grad.dtype),
        compiler_params=params(),
        cost_estimate=cost(0, 4 * share * breadth * width),
        name="cut_share",
    )(grad, *after)


def block_part(grad, rims, weights, tops, unit):
    height, breadth, filters = grad.shape
    depth = weights.shape[1] // 3
    span, count = unit * breadth, len(tops)
    lane = min(depth, LANES)

    def body(inputs, out_refs, scratch):
        grad_any, rims_any, weights_any = inputs
        (out_ref,) = out_refs
        grads, taps, sums, results, g_sem, r_sem, w_sem, o_sem = scratch

        def rows_of(n):
            top = tops[n]
            low, high = max(top - 1, 0), min(top + unit + 1, height)
            copies = [
                pltpu.make_async_copy(
                    grad_any.at[pl.ds(low, high - low)],
                    grads.at[n, pl.ds(low - top + 1, high - low)],
                    g_sem.at[n],
                )
            ]
            for e, edge in enumerate((low == top, high == top + unit)):
                if edge:
                    copies.append(
                        pltpu.make_async_copy(
                            rims_any.at[pl.ds(e, 1)],
                            grads.at[n, pl.ds(e * (unit + 1), 1)],
                            r_sem.at[n, e],
                        )
                    )
            return copies

        loads = [
            pltpu.make_async_copy(
                weights_any.at[r, pl.ds(s * depth, depth)],
                taps.at[r, pl.ds(s * depth, depth)],
                w_sem.at[r, s],
            )
            for r in range(3)
            for s in range(3)
        ]
        groups = [rows_of(0) + loads[:1], loads[1:3], loads[3:6], loads[6:]]
        groups += [rows_of(n) for n in range(1, count)]
        stream = Stream(groups, 2)
        yield
        waits = {0: 0, 1: 1, 3: 2, 6: 3}
        column = lax.broadcasted_iota(jnp.int32, (unit, breadth, lane), 1).reshape(span, lane)
        stores = []
        for n, top in enumerate(tops):
            if n > 0:
                stream.wait(3 + n)
            for r in range(3):
                for s in range(3):
                    if n == 0 and 3 * r + s in waits:
                        stream.wait(waits[3 * r + s])
                    moved = grads[n, 2 - r : 2 - r + unit].reshape(span, filters)
                    product = lax.dot_general(
                        moved,
                        taps[r, s * depth : (s + 1) * depth, :],
                        (((1,), (1,)), ((), ())),
                        preferred_element_type=jnp.float32,
                    )
                    if r == 0:
                        sums[s] = product
                    else:
                        sums[s] += product
            for low in range(0, depth, lane):
                before = pltpu.roll(sums[2, :, low : low + lane], 1, 0)
                behind = pltpu.roll(sums[0, :, low : low + lane], span - 1, 0)
                value = (
                    sums[1, :, low : low + lane]
                    + jnp.where(column == 0, 0.0, before)
                    + jnp.where(column == breadth - 1, 0.0, behind)
                )
                results[n, :, :, low : low + lane] = value.astype(jnp.bfloat16).reshape(
                    unit, breadth, lane
                )
            stores.append(
                pltpu.make_async_copy(results.at[n], out_ref.at[pl.ds(n * unit, unit)], o_sem.at[n])
            )
            stores[-1].start()
        for c in stores:
            c.wait()

    shape = jax.ShapeDtypeStruct((count * unit, breadth, depth), jnp.bfloat16)
    return Part(
        body,
        [grad, rims, weights],
        [(shape, ANY)],
        [
            pltpu.VMEM((count, unit + 2, breadth, filters), jnp.bfloat16),
            pltpu.VMEM(weights.shape, jnp.bfloat16),
            pltpu.VMEM((3, span, depth), jnp.float32),
            pltpu.VMEM((count, unit, breadth, depth), jnp.bfloat16),
            pltpu.SemaphoreType.DMA((count,)),
            pltpu.SemaphoreType.DMA((count, 2)),
            pltpu.SemaphoreType.DMA((3, 3)),
            pltpu.SemaphoreType.DMA((count,)),
        ],
        (18 * count * unit * breadth * depth * filters, 2 * weights.size),
    )


def per_device(saved_input, upstream, kernel):
    height, breadth, filters = upstream.shape
    part = saved_input.shape[1]
    channels = kernel.shape[2]
    tiles, chans, filts = (lax.axis_size(a) for a in ("tile", "chan", "filt"))
    tile, filt = (lax.axis_index(a) for a in ("tile", "filt"))
    depth = channels // tiles

    def chunk(bits, saved=saved_input):
        return lax.dynamic_slice_in_dim(saved, (tile ^ bits) * depth, depth, axis=2)

    def columns(value):
        if filts == 2:
            return [value, swap(value, "filt", 1)]
        return [lax.all_gather(value, "filt", axis=1, tiled=True)]

    sent_far = chunk(2)
    pair_far = swap(sent_far, "tile", 1)
    own_far = columns(chunk(3))

    even = tile % 2 == 0
    first, last = upstream[:1], upstream[height - 1 :]
    up = [(i, i + 1) for i in range(tiles - 1)]
    inward, outward = jnp.where(even, last, first), jnp.where(even, first, last)
    above = lax.ppermute(last, "tile", up)
    below = lax.ppermute(first, "tile", [(j, i) for i, j in up])
    across = lax.ppermute(outward, "tile", [(1, 3), (2, 0)])
    rims = jnp.concatenate(
        [above, below, jnp.where(even, inward, across), jnp.where(even, across, inward)], axis=0
    )

    weights = kernel.reshape(3, 3 * channels, filters)
    unit = largest(height, 16)
    tops = list(range(0, height, unit))
    halves = [h for h in (tops[:1], tops[1:]) if h]
    partials = []

    def next_rows(after):
        part_ = block_part(upstream, rims, weights, halves[len(partials)], unit)
        ((partial,),) = run("block_grad", [part_], after)
        partials.append(partial)
        return [partial]

    if chans == 4 and filters % (4 * LANES) == 0 and height % 2 == 0:
        share, width = height // 2, filters // 4
        near_cut = cut_share(upstream, 0, share, width, [pair_far, rims])
        far_cut = cut_share(upstream, 1, share, width, [near_cut])
        own_far = shifted_active(own_far, [far_cut])
        fetched = [swap(near_cut, "tile", 1), swap(far_cut, "tile", 1)]
        pair_far = shifted_active(columns(pair_far), [own_far])
        fetched[0], _ = lax.optimization_barrier((fetched[0], pair_far))
        crossed = [swap(v, "chan", 2) for v in fetched]
        pieces = [[v, swap(v, "chan", 1)] for v in fetched]

        def place_of(j):
            return lambda: (lax.axis_index("chan") // 2 ^ (j // 2)) * 2 + j % 2

        def order(k):
            return lax.axis_index("chan") % 2 ^ k

        groups = [[0], [1], [2, 3]]
    else:
        own_far = shifted_active(own_far, [])
        pair_far = shifted_active(columns(pair_far), [own_far])
        crossed, pieces = [], [[swap(upstream, "tile", 1)]]

        def place_of(j):
            return lambda: 0

        def order(k):
            return 0

        groups = [[0]]
    chain = [pair_far]
    arrived = []
    saved, _ = lax.optimization_barrier((saved_input, pair_far))
    pair_near = swap(chunk(1, saved), "tile", 1)
    for n, group in enumerate(groups):
        if n == 2:
            pieces += [[v, swap(v, "chan", 1)] for v in crossed]
        blocks = [(place_of(j), v) for j, v in enumerate(pieces)]
        sums = sums_part(
            [blocks[j] for j in group], order, (own_far, 0), (pair_far, 0), upstream, rims
        )
        (far,) = run("kernel_sums", [sums], chain)
        chain = [far[-1]]
        arrived += [swap(v, "tile", 3) for v in far]
        if n == 0:
            pair_near, _ = lax.optimization_barrier((pair_near, far[0]))
            near = columns(jnp.concatenate([chunk(0), pair_near], axis=0))
            chain = next_rows(chain)
    partials[0], _ = lax.optimization_barrier((partials[0], far[-1]))
    while len(partials) < len(halves):
        chain = next_rows(chain)
    near = shifted_active(near, chain)
    early = len(arrived) // 2
    last = sums_part(blocks, order, (near, 0), (near, 1), upstream, rims, arrived[:early], filters)
    ((out,),) = run("kernel_sums", [last], [near])
    summed = []
    for partial in partials:
        if filts == 2:
            mine = lax.dynamic_slice_in_dim(partial, filt * part, part, axis=1)
            other = lax.dynamic_slice_in_dim(partial, (1 - filt) * part, part, axis=1)
            total = mine.astype(jnp.float32) + swap(other, "filt", 1).astype(jnp.float32)
        else:
            total = lax.psum_scatter(partial, "filt", scatter_dimension=1, tiled=True).astype(
                jnp.float32
            )
        summed.append(total)
    masked = jnp.where(saved_input > 0, jnp.concatenate(summed, 0), jnp.zeros((), jnp.float32))
    input_grad = masked.astype(jnp.bfloat16)
    places = [place for place, _ in blocks[early:]]
    out = add_blocks(places, arrived[early:], out, [input_grad])
    return input_grad, out.reshape(3, 3, depth, filters)


def solution(mesh):
    placed = (P("tile", "filt", "chan"), P("tile", None, "filt"), P(None, None, "chan", "filt"))
    return jax.shard_map(
        per_device,
        mesh=mesh,
        in_specs=placed,
        out_specs=(P("tile", "filt", "chan"), P(None, None, ("chan", "tile"), "filt")),
        check_vma=False,
    )
```

```python
import dataclasses
from collections.abc import Callable

import jax
import jax.numpy as jnp
from jax import lax
from jax.experimental import pallas as pl
from jax.experimental.pallas import tpu as pltpu
from jax.sharding import PartitionSpec as P

LANES = 128
VMEM = 62 << 20
ANY = pl.BlockSpec(memory_space=pl.ANY)


def largest(total, most):
    return max(n for n in range(1, most + 1) if total % n == 0)


def cost(flops, moved):
    return pl.CostEstimate(flops=flops * 8, bytes_accessed=moved * 8, transcendentals=0)


def params():
    return pltpu.CompilerParams(vmem_limit_bytes=VMEM)


def swap(value, axis, bit):
    count = lax.axis_size(axis)
    return lax.ppermute(value, axis, [(i, i ^ bit) for i in range(count)])


class Stream:
    def __init__(self, groups, ahead):
        self.groups, self.ahead, self.begun = groups, ahead, 0
        self.begin(ahead)

    def begin(self, upto):
        while self.begun < min(upto, len(self.groups)):
            for copy in self.groups[self.begun]:
                copy.start()
            self.begun += 1

    def wait(self, k):
        for copy in self.groups[k]:
            copy.wait()
        self.begin(k + 1 + self.ahead)


@dataclasses.dataclass
class Part:
    body: Callable
    operands: list
    outs: list
    scratch: list
    work: tuple


def run(name, parts, after):
    ins = [len(p.operands) for p in parts]
    outs = [len(p.outs) for p in parts]
    scratch = [len(p.scratch) for p in parts]

    def split(refs, counts):
        lists, at = [], 0
        for n in counts:
            lists.append(refs[at : at + n])
            at += n
        return lists

    def body(*refs):
        first = sum(ins) + len(after)
        inputs = split(refs[: sum(ins)], ins)
        results = split(refs[first : first + sum(outs)], outs)
        held = split(refs[first + sum(outs) :], scratch)
        steps = [p.body(i, o, h) for p, i, o, h in zip(parts, inputs, results, held)]
        for step in steps:
            next(step)
        for step in steps:
            for _ in step:
                pass

    flat = pl.pallas_call(
        body,
        in_specs=[ANY] * (sum(ins) + len(after)),
        out_specs=[spec for p in parts for _, spec in p.outs],
        scratch_shapes=[x for p in parts for x in p.scratch],
        out_shape=[shape for p in parts for shape, _ in p.outs],
        compiler_params=params(),
        cost_estimate=cost(sum(p.work[0] for p in parts), sum(p.work[1] for p in parts)),
        name=name,
    )(*[x for p in parts for x in p.operands], *after)
    return split(flat, outs)


def shifted_active(parts, after):
    height, part, depth = parts[0].shape
    breadth = part * len(parts)
    rows = largest(height, 32)
    span = rows * breadth

    def body(*refs):
        part_refs, out_ref = refs[: len(parts)], refs[-1]
        read = [jnp.maximum(ref[...].astype(jnp.float32), 0.0) for ref in part_refs]
        whole = read[0]
        if len(read) == 2:
            whole = jnp.where(
                lax.axis_index("filt") == 0,
                jnp.concatenate(read, 1),
                jnp.concatenate(read[::-1], 1),
            )
        active = whole.reshape(span, depth).T
        column = lax.broadcasted_iota(jnp.int32, (1, span), 1) % breadth
        before = jnp.where(column == 0, 0.0, pltpu.roll(active, 1, 1))
        behind = jnp.where(column == breadth - 1, 0.0, pltpu.roll(active, span - 1, 1))
        out_ref[0] = before.astype(jnp.bfloat16)
        out_ref[1] = active.astype(jnp.bfloat16)
        out_ref[2] = behind.astype(jnp.bfloat16)

    return pl.pallas_call(
        body,
        grid=(height // rows,),
        in_specs=[pl.BlockSpec((rows, part, depth), lambda i: (i, 0, 0))] * len(parts)
        + [ANY] * len(after),
        out_specs=pl.BlockSpec((3, depth, span), lambda i: (0, 0, i)),
        out_shape=jax.ShapeDtypeStruct((3, depth, height * breadth), jnp.bfloat16),
        compiler_params=params(),
        cost_estimate=cost(0, 8 * height * breadth * depth),
        name="shifted_active",
    )(*parts, *after)


def column_slice(index, width):
    start = index * width
    return pl.ds(pl.multiple_of(start, width) if width % LANES == 0 else start, width)


def sums_part(blocks, order, own, pair, own_grad, rims, arrived=(), full=None):
    (own_active, own_at), (pair_active, pair_at) = own, pair
    depth = own_active.shape[1]
    parts, count = len(blocks[0][1]), len(blocks)
    share, breadth, width = blocks[0][1][0].shape
    height = share * parts
    total = width * count
    cuts = [[0, height // 4, height], [0, height]] if height % 4 == 0 else [[0, height]] * 2
    waits = sum(len(c) - 1 for c in cuts)
    dtype = jnp.bfloat16 if full is None else jnp.float32
    outs = count if full is None else 1

    def body(inputs, out_refs, scratch):
        own_a, pair_a, own_g, rims_ref, *refs = inputs
        pieces = [refs[parts * b : parts * (b + 1)] for b in range(count)]
        arrived_refs = refs[parts * count :]
        actives, grads, sums, came, a_sem, g_sem, r_sem, p_sem, c_sem, o_sem = scratch
        columns = [column_slice(place(), width) for place, _ in blocks]
        held = [pl.ds(b * width, width) for b in range(count)]

        def load(t, k, low, high):
            group = []
            if low == 0:
                for b in range(count):
                    for e in range(2):
                        group.append(
                            pltpu.make_async_copy(
                                rims_ref.at[pl.ds(2 * t + e, 1), :, columns[b]],
                                grads.at[t, pl.ds(e * (height + 1), 1), :, held[b]],
                                r_sem.at[t, b, e],
                            )
                        )
            if t == 0:
                first, last = low + (low > 0), min(high + 1, height)
                for b in range(count):
                    group.append(
                        pltpu.make_async_copy(
                            own_g.at[pl.ds(first, last - first), :, columns[b]],
                            grads.at[0, pl.ds(first + 1, last - first), :, held[b]],
                            g_sem.at[k, b],
                        )
                    )
            elif low == 0:
                for b in range(count):
                    for k_piece in range(parts):
                        group.append(
                            pltpu.make_async_copy(
                                pieces[b][k_piece],
                                grads.at[1, pl.ds(order(k_piece) * share + 1, share), :, held[b]],
                                p_sem.at[b, k_piece],
                            )
                        )
            ref, at = ((own_a, own_at), (pair_a, pair_at))[t]
            group.append(
                pltpu.make_async_copy(
                    ref.at[:, :, pl.ds((at * height + low) * breadth, (high - low) * breadth)],
                    actives.at[t, :, :, pl.ds(low * breadth, (high - low) * breadth)],
                    a_sem.at[t, k],
                )
            )
            return group

        spans = [
            (t, k, cuts[t][k], cuts[t][k + 1]) for t in range(2) for k in range(len(cuts[t]) - 1)
        ]
        groups = [load(*span) for span in spans]
        groups[-1] += [
            pltpu.make_async_copy(ref, came.at[:, :, held[b]], c_sem.at[b])
            for b, ref in enumerate(arrived_refs)
        ]
        stream = Stream(groups, 2)
        yield
        for n, (t, k, low, high) in enumerate(spans):
            stream.wait(n)
            active = actives[t, :, :, low * breadth : high * breadth]
            active = active.reshape(3 * depth, (high - low) * breadth)
            for r in range(3):
                grad = grads[t, low + 2 - r : high + 2 - r].reshape((high - low) * breadth, total)
                product = jnp.dot(active, grad, preferred_element_type=jnp.float32)
                if n > 0:
                    product += sums[r]
                if n == waits - 1 and arrived:
                    known = width * len(arrived)
                    extra = came[r, :, :known].astype(jnp.float32)
                    sums[r, :, :known] = product[:, :known] + extra
                    sums[r, :, known:] = product[:, known:]
                elif n == waits - 1 and full is None:
                    for b in range(count):
                        out_refs[b][r] = product[:, b * width : (b + 1) * width].astype(dtype)
                else:
                    sums[r] = product
        if full is not None:
            stores = [
                pltpu.make_async_copy(
                    sums.at[:, :, held[b]], out_refs[0].at[:, :, columns[b]], o_sem.at[b]
                )
                for b in range(count)
            ]
            for c in stores:
                c.start()
            for c in stores:
                c.wait()

    moved = 2 * (6 * depth + 2 * total) * height * breadth + 9 * depth * total * 4
    operands = [own_active, pair_active, own_grad, rims]
    operands += [piece for _, grads in blocks for piece in grads] + list(arrived)
    shape = jax.ShapeDtypeStruct((3, 3 * depth, full or width), dtype)
    return Part(
        body,
        operands,
        [(shape, pl.BlockSpec(memory_space=pltpu.VMEM) if full is None else ANY)] * outs,
        [
            pltpu.VMEM((2, 3, depth, height * breadth), jnp.bfloat16),
            pltpu.VMEM((2, height + 2, breadth, total), jnp.bfloat16),
            pltpu.VMEM((3, 3 * depth, total), jnp.float32),
            pltpu.VMEM((3, 3 * depth, total if arrived else LANES), jnp.bfloat16),
            pltpu.SemaphoreType.DMA((2, waits)),
            pltpu.SemaphoreType.DMA((waits, count)),
            pltpu.SemaphoreType.DMA((2, count, 2)),
            pltpu.SemaphoreType.DMA((count, parts)),
            pltpu.SemaphoreType.DMA((count,)),
            pltpu.SemaphoreType.DMA((count,)),
        ],
        (4 * 9 * depth * total * height * breadth, moved),
    )


def add_blocks(places, arrived, out, after):
    taps, depth, width = arrived[0].shape
    count = len(arrived)

    def body(*refs):
        arrived_refs = refs[:count]
        out_ref, came, held, sems = refs[-4:]
        steps = [(b, k) for b in range(count) for k in range(taps)]
        columns = [column_slice(place(), width) for place in places]

        def there(b, k):
            return out_ref.at[k, :, columns[b]]

        loads = [
            (
                pltpu.make_async_copy(arrived_refs[b].at[k], came.at[b, k], sems.at[0, b, k]),
                pltpu.make_async_copy(there(b, k), held.at[b, k], sems.at[1, b, k]),
            )
            for b, k in steps
        ]
        stores = [
            pltpu.make_async_copy(held.at[b, k], there(b, k), sems.at[2, b, k]) for b, k in steps
        ]
        for pair in loads:
            for c in pair:
                c.start()
        for n, (b, k) in enumerate(steps):
            for c in loads[n]:
                c.wait()
            held[b, k] += came[b, k].astype(jnp.float32)
            stores[n].start()
        for c in stores:
            c.wait()

    return pl.pallas_call(
        body,
        in_specs=[ANY] * (count + 1 + len(after)),
        out_specs=ANY,
        scratch_shapes=[
            pltpu.VMEM((count, taps, depth, width), jnp.bfloat16),
            pltpu.VMEM((count, taps, depth, width), jnp.float32),
            pltpu.SemaphoreType.DMA((3, count, taps)),
        ],
        out_shape=jax.ShapeDtypeStruct(out.shape, jnp.float32),
        input_output_aliases={count: 0},
        compiler_params=params(),
        cost_estimate=cost(count * taps * depth * width, 10 * count * taps * depth * width),
        name="add_blocks",
    )(*arrived, out, *after)


def cut_share(grad, block, share, width, after):
    breadth = grad.shape[1]

    def body(grad_ref, *refs):
        out_ref, sem = refs[-2:]
        chan = lax.axis_index("chan")
        load = pltpu.make_async_copy(
            grad_ref.at[
                pl.ds(chan % 2 * share, share), :, column_slice(chan // 2 * 2 + block, width)
            ],
            out_ref,
            sem,
        )
        load.start()
        load.wait()

    return pl.pallas_call(
        body,
        in_specs=[ANY] * (1 + len(after)),
        out_specs=pl.BlockSpec(memory_space=pltpu.VMEM),
        scratch_shapes=[pltpu.SemaphoreType.DMA],
        out_shape=jax.ShapeDtypeStruct((share, breadth, width), grad.dtype),
        compiler_params=params(),
        cost_estimate=cost(0, 4 * share * breadth * width),
        name="cut_share",
    )(grad, *after)


def block_part(grad, rims, weights, tops, unit):
    height, breadth, filters = grad.shape
    depth = weights.shape[1] // 3
    span, count = unit * breadth, len(tops)
    lane = min(depth, LANES)

    def body(inputs, out_refs, scratch):
        grad_any, rims_any, weights_any = inputs
        (out_ref,) = out_refs
        grads, taps, sums, results, g_sem, r_sem, w_sem, o_sem = scratch

        def rows_of(n):
            top = tops[n]
            low, high = max(top - 1, 0), min(top + unit + 1, height)
            copies = [
                pltpu.make_async_copy(
                    grad_any.at[pl.ds(low, high - low)],
                    grads.at[n, pl.ds(low - top + 1, high - low)],
                    g_sem.at[n],
                )
            ]
            for e, edge in enumerate((low == top, high == top + unit)):
                if edge:
                    copies.append(
                        pltpu.make_async_copy(
                            rims_any.at[pl.ds(e, 1)],
                            grads.at[n, pl.ds(e * (unit + 1), 1)],
                            r_sem.at[n, e],
                        )
                    )
            return copies

        loads = [
            pltpu.make_async_copy(
                weights_any.at[r, pl.ds(s * depth, depth)],
                taps.at[r, pl.ds(s * depth, depth)],
                w_sem.at[r, s],
            )
            for r in range(3)
            for s in range(3)
        ]
        groups = [rows_of(0) + loads[:1], loads[1:3], loads[3:6], loads[6:]]
        groups += [rows_of(n) for n in range(1, count)]
        stream = Stream(groups, 2)
        yield
        waits = {0: 0, 1: 1, 3: 2, 6: 3}
        column = lax.broadcasted_iota(jnp.int32, (unit, breadth, lane), 1).reshape(span, lane)
        stores = []
        for n, top in enumerate(tops):
            if n > 0:
                stream.wait(3 + n)
            for r in range(3):
                for s in range(3):
                    if n == 0 and 3 * r + s in waits:
                        stream.wait(waits[3 * r + s])
                    moved = grads[n, 2 - r : 2 - r + unit].reshape(span, filters)
                    product = lax.dot_general(
                        moved,
                        taps[r, s * depth : (s + 1) * depth, :],
                        (((1,), (1,)), ((), ())),
                        preferred_element_type=jnp.float32,
                    )
                    if r == 0:
                        sums[s] = product
                    else:
                        sums[s] += product
            for low in range(0, depth, lane):
                before = pltpu.roll(sums[2, :, low : low + lane], 1, 0)
                behind = pltpu.roll(sums[0, :, low : low + lane], span - 1, 0)
                value = (
                    sums[1, :, low : low + lane]
                    + jnp.where(column == 0, 0.0, before)
                    + jnp.where(column == breadth - 1, 0.0, behind)
                )
                results[n, :, :, low : low + lane] = value.astype(jnp.bfloat16).reshape(
                    unit, breadth, lane
                )
            stores.append(
                pltpu.make_async_copy(results.at[n], out_ref.at[pl.ds(n * unit, unit)], o_sem.at[n])
            )
            stores[-1].start()
        for c in stores:
            c.wait()

    shape = jax.ShapeDtypeStruct((count * unit, breadth, depth), jnp.bfloat16)
    return Part(
        body,
        [grad, rims, weights],
        [(shape, ANY)],
        [
            pltpu.VMEM((count, unit + 2, breadth, filters), jnp.bfloat16),
            pltpu.VMEM(weights.shape, jnp.bfloat16),
            pltpu.VMEM((3, span, depth), jnp.float32),
            pltpu.VMEM((count, unit, breadth, depth), jnp.bfloat16),
            pltpu.SemaphoreType.DMA((count,)),
            pltpu.SemaphoreType.DMA((count, 2)),
            pltpu.SemaphoreType.DMA((3, 3)),
            pltpu.SemaphoreType.DMA((count,)),
        ],
        (18 * count * unit * breadth * depth * filters, 2 * weights.size),
    )


def per_device(saved_input, upstream, kernel):
    height, breadth, filters = upstream.shape
    part = saved_input.shape[1]
    channels = kernel.shape[2]
    tiles, chans, filts = (lax.axis_size(a) for a in ("tile", "chan", "filt"))
    tile, filt = (lax.axis_index(a) for a in ("tile", "filt"))
    depth = channels // tiles

    def chunk(bits, saved=saved_input):
        return lax.dynamic_slice_in_dim(saved, (tile ^ bits) * depth, depth, axis=2)

    def columns(value):
        if filts == 2:
            return [value, swap(value, "filt", 1)]
        return [lax.all_gather(value, "filt", axis=1, tiled=True)]

    sent_far = chunk(2)
    pair_far = swap(sent_far, "tile", 1)
    own_far = columns(chunk(3))

    even = tile % 2 == 0
    first, last = upstream[:1], upstream[height - 1 :]
    up = [(i, i + 1) for i in range(tiles - 1)]
    inward, outward = jnp.where(even, last, first), jnp.where(even, first, last)
    above = lax.ppermute(last, "tile", up)
    below = lax.ppermute(first, "tile", [(j, i) for i, j in up])
    across = lax.ppermute(outward, "tile", [(1, 3), (2, 0)])
    rims = jnp.concatenate(
        [above, below, jnp.where(even, inward, across), jnp.where(even, across, inward)], axis=0
    )

    weights = kernel.reshape(3, 3 * channels, filters)
    unit = largest(height, 16)
    tops = list(range(0, height, unit))
    halves = [h for h in (tops[:1], tops[1:]) if h]
    partials = []

    def next_rows(after):
        part_ = block_part(upstream, rims, weights, halves[len(partials)], unit)
        ((partial,),) = run("block_grad", [part_], after)
        partials.append(partial)
        return [partial]

    if chans == 4 and filters % (4 * LANES) == 0 and height % 2 == 0:
        share, width = height // 2, filters // 4
        near_cut = cut_share(upstream, 0, share, width, [pair_far, rims, *own_far])
        far_cut = cut_share(upstream, 1, share, width, [near_cut])
        own_far = shifted_active(own_far, [far_cut])
        fetched = [swap(near_cut, "tile", 1), swap(far_cut, "tile", 1)]
        pair_far = shifted_active(columns(pair_far), [own_far])
        fetched[0], _ = lax.optimization_barrier((fetched[0], pair_far))
        crossed = [swap(v, "chan", 2) for v in fetched]
        pieces = [[v, swap(v, "chan", 1)] for v in fetched]

        def place_of(j):
            return lambda: (lax.axis_index("chan") // 2 ^ (j // 2)) * 2 + j % 2

        def order(k):
            return lax.axis_index("chan") % 2 ^ k

        groups = [[0], [1], [2, 3]]
    else:
        own_far = shifted_active(own_far, [])
        pair_far = shifted_active(columns(pair_far), [own_far])
        crossed, pieces = [], [[swap(upstream, "tile", 1)]]

        def place_of(j):
            return lambda: 0

        def order(k):
            return 0

        groups = [[0]]
    chain = [pair_far]
    arrived = []
    saved, _ = lax.optimization_barrier((saved_input, pair_far))
    pair_near = swap(chunk(1, saved), "tile", 1)
    for n, group in enumerate(groups):
        if n == 2:
            pieces += [[v, swap(v, "chan", 1)] for v in crossed]
        blocks = [(place_of(j), v) for j, v in enumerate(pieces)]
        sums = sums_part(
            [blocks[j] for j in group], order, (own_far, 0), (pair_far, 0), upstream, rims
        )
        (far,) = run("kernel_sums", [sums], chain)
        chain = [far[-1]]
        arrived += [swap(v, "tile", 3) for v in far]
        if n == 0:
            pair_near, _ = lax.optimization_barrier((pair_near, far[0]))
            near = columns(jnp.concatenate([chunk(0), pair_near], axis=0))
            chain = next_rows(chain)
    while len(partials) < len(halves):
        chain = next_rows(chain)
    near = shifted_active(near, chain)
    early = len(arrived) // 2
    last = sums_part(blocks, order, (near, 0), (near, 1), upstream, rims, arrived[:early], filters)
    ((out,),) = run("kernel_sums", [last], [near])
    summed = []
    for partial in partials:
        if filts == 2:
            mine = lax.dynamic_slice_in_dim(partial, filt * part, part, axis=1)
            other = lax.dynamic_slice_in_dim(partial, (1 - filt) * part, part, axis=1)
            total = mine.astype(jnp.float32) + swap(other, "filt", 1).astype(jnp.float32)
        else:
            total = lax.psum_scatter(partial, "filt", scatter_dimension=1, tiled=True).astype(
                jnp.float32
            )
        summed.append(total)
    masked = jnp.where(saved_input > 0, jnp.concatenate(summed, 0), jnp.zeros((), jnp.float32))
    input_grad = masked.astype(jnp.bfloat16)
    places = [place for place, _ in blocks[early:]]
    out = add_blocks(places, arrived[early:], out, [input_grad])
    return input_grad, out.reshape(3, 3, depth, filters)


def solution(mesh):
    placed = (P("tile", "filt", "chan"), P("tile", None, "filt"), P(None, None, "chan", "filt"))
    return jax.shard_map(
        per_device,
        mesh=mesh,
        in_specs=placed,
        out_specs=(P("tile", "filt", "chan"), P(None, None, ("chan", "tile"), "filt")),
        check_vma=False,
    )
```

```python
import dataclasses
from collections.abc import Callable

import jax
import jax.numpy as jnp
from jax import lax
from jax.experimental import pallas as pl
from jax.experimental.pallas import tpu as pltpu
from jax.sharding import PartitionSpec as P

LANES = 128
VMEM = 62 << 20
ANY = pl.BlockSpec(memory_space=pl.ANY)


def largest(total, most):
    return max(n for n in range(1, most + 1) if total % n == 0)


def cost(flops, moved):
    return pl.CostEstimate(flops=flops * 8, bytes_accessed=moved * 8, transcendentals=0)


def params():
    return pltpu.CompilerParams(vmem_limit_bytes=VMEM)


def swap(value, axis, bit):
    count = lax.axis_size(axis)
    return lax.ppermute(value, axis, [(i, i ^ bit) for i in range(count)])


class Stream:
    def __init__(self, groups, ahead):
        self.groups, self.ahead, self.begun = groups, ahead, 0
        self.begin(ahead)

    def begin(self, upto):
        while self.begun < min(upto, len(self.groups)):
            for copy in self.groups[self.begun]:
                copy.start()
            self.begun += 1

    def wait(self, k):
        for copy in self.groups[k]:
            copy.wait()
        self.begin(k + 1 + self.ahead)


@dataclasses.dataclass
class Part:
    body: Callable
    operands: list
    outs: list
    scratch: list
    work: tuple


def run(name, parts, after):
    ins = [len(p.operands) for p in parts]
    outs = [len(p.outs) for p in parts]
    scratch = [len(p.scratch) for p in parts]

    def split(refs, counts):
        lists, at = [], 0
        for n in counts:
            lists.append(refs[at : at + n])
            at += n
        return lists

    def body(*refs):
        first = sum(ins) + len(after)
        inputs = split(refs[: sum(ins)], ins)
        results = split(refs[first : first + sum(outs)], outs)
        held = split(refs[first + sum(outs) :], scratch)
        steps = [p.body(i, o, h) for p, i, o, h in zip(parts, inputs, results, held)]
        for step in steps:
            next(step)
        for step in steps:
            for _ in step:
                pass

    flat = pl.pallas_call(
        body,
        in_specs=[ANY] * (sum(ins) + len(after)),
        out_specs=[spec for p in parts for _, spec in p.outs],
        scratch_shapes=[x for p in parts for x in p.scratch],
        out_shape=[shape for p in parts for shape, _ in p.outs],
        compiler_params=params(),
        cost_estimate=cost(sum(p.work[0] for p in parts), sum(p.work[1] for p in parts)),
        name=name,
    )(*[x for p in parts for x in p.operands], *after)
    return split(flat, outs)


def shifted_active(parts, after):
    height, part, depth = parts[0].shape
    breadth = part * len(parts)
    rows = largest(height, 32)
    span = rows * breadth

    def body(*refs):
        part_refs, out_ref = refs[: len(parts)], refs[-1]
        read = [jnp.maximum(ref[...].astype(jnp.float32), 0.0) for ref in part_refs]
        whole = read[0]
        if len(read) == 2:
            whole = jnp.where(
                lax.axis_index("filt") == 0,
                jnp.concatenate(read, 1),
                jnp.concatenate(read[::-1], 1),
            )
        active = whole.reshape(span, depth).T
        column = lax.broadcasted_iota(jnp.int32, (1, span), 1) % breadth
        before = jnp.where(column == 0, 0.0, pltpu.roll(active, 1, 1))
        behind = jnp.where(column == breadth - 1, 0.0, pltpu.roll(active, span - 1, 1))
        out_ref[0] = before.astype(jnp.bfloat16)
        out_ref[1] = active.astype(jnp.bfloat16)
        out_ref[2] = behind.astype(jnp.bfloat16)

    return pl.pallas_call(
        body,
        grid=(height // rows,),
        in_specs=[pl.BlockSpec((rows, part, depth), lambda i: (i, 0, 0))] * len(parts)
        + [ANY] * len(after),
        out_specs=pl.BlockSpec((3, depth, span), lambda i: (0, 0, i)),
        out_shape=jax.ShapeDtypeStruct((3, depth, height * breadth), jnp.bfloat16),
        compiler_params=params(),
        cost_estimate=cost(0, 8 * height * breadth * depth),
        name="shifted_active",
    )(*parts, *after)


def column_slice(index, width):
    start = index * width
    return pl.ds(pl.multiple_of(start, width) if width % LANES == 0 else start, width)


def sums_part(blocks, order, own, pair, own_grad, rims, arrived=(), full=None):
    (own_active, own_at), (pair_active, pair_at) = own, pair
    depth = own_active.shape[1]
    parts, count = len(blocks[0][1]), len(blocks)
    share, breadth, width = blocks[0][1][0].shape
    height = share * parts
    total = width * count
    cuts = [[0, height // 4, height], [0, height]] if height % 4 == 0 else [[0, height]] * 2
    waits = sum(len(c) - 1 for c in cuts)
    dtype = jnp.bfloat16 if full is None else jnp.float32
    outs = count if full is None else 1

    def body(inputs, out_refs, scratch):
        own_a, pair_a, own_g, rims_ref, *refs = inputs
        pieces = [refs[parts * b : parts * (b + 1)] for b in range(count)]
        arrived_refs = refs[parts * count :]
        actives, grads, sums, came, a_sem, g_sem, r_sem, p_sem, c_sem, o_sem = scratch
        columns = [column_slice(place(), width) for place, _ in blocks]
        held = [pl.ds(b * width, width) for b in range(count)]

        def load(t, k, low, high):
            group = []
            if low == 0:
                for b in range(count):
                    for e in range(2):
                        group.append(
                            pltpu.make_async_copy(
                                rims_ref.at[pl.ds(2 * t + e, 1), :, columns[b]],
                                grads.at[t, pl.ds(e * (height + 1), 1), :, held[b]],
                                r_sem.at[t, b, e],
                            )
                        )
            if t == 0:
                first, last = low + (low > 0), min(high + 1, height)
                for b in range(count):
                    group.append(
                        pltpu.make_async_copy(
                            own_g.at[pl.ds(first, last - first), :, columns[b]],
                            grads.at[0, pl.ds(first + 1, last - first), :, held[b]],
                            g_sem.at[k, b],
                        )
                    )
            elif low == 0:
                for b in range(count):
                    for k_piece in range(parts):
                        group.append(
                            pltpu.make_async_copy(
                                pieces[b][k_piece],
                                grads.at[1, pl.ds(order(k_piece) * share + 1, share), :, held[b]],
                                p_sem.at[b, k_piece],
                            )
                        )
            ref, at = ((own_a, own_at), (pair_a, pair_at))[t]
            group.append(
                pltpu.make_async_copy(
                    ref.at[:, :, pl.ds((at * height + low) * breadth, (high - low) * breadth)],
                    actives.at[t, :, :, pl.ds(low * breadth, (high - low) * breadth)],
                    a_sem.at[t, k],
                )
            )
            return group

        spans = [
            (t, k, cuts[t][k], cuts[t][k + 1]) for t in range(2) for k in range(len(cuts[t]) - 1)
        ]
        groups = [load(*span) for span in spans]
        groups[-1] += [
            pltpu.make_async_copy(ref, came.at[:, :, held[b]], c_sem.at[b])
            for b, ref in enumerate(arrived_refs)
        ]
        stream = Stream(groups, 2)
        yield
        for n, (t, k, low, high) in enumerate(spans):
            stream.wait(n)
            active = actives[t, :, :, low * breadth : high * breadth]
            active = active.reshape(3 * depth, (high - low) * breadth)
            for r in range(3):
                grad = grads[t, low + 2 - r : high + 2 - r].reshape((high - low) * breadth, total)
                product = jnp.dot(active, grad, preferred_element_type=jnp.float32)
                if n > 0:
                    product += sums[r]
                if n == waits - 1 and arrived:
                    known = width * len(arrived)
                    extra = came[r, :, :known].astype(jnp.float32)
                    sums[r, :, :known] = product[:, :known] + extra
                    sums[r, :, known:] = product[:, known:]
                elif n == waits - 1 and full is None:
                    for b in range(count):
                        out_refs[b][r] = product[:, b * width : (b + 1) * width].astype(dtype)
                else:
                    sums[r] = product
        if full is not None:
            stores = [
                pltpu.make_async_copy(
                    sums.at[:, :, held[b]], out_refs[0].at[:, :, columns[b]], o_sem.at[b]
                )
                for b in range(count)
            ]
            for c in stores:
                c.start()
            for c in stores:
                c.wait()

    moved = 2 * (6 * depth + 2 * total) * height * breadth + 9 * depth * total * 4
    operands = [own_active, pair_active, own_grad, rims]
    operands += [piece for _, grads in blocks for piece in grads] + list(arrived)
    shape = jax.ShapeDtypeStruct((3, 3 * depth, full or width), dtype)
    return Part(
        body,
        operands,
        [(shape, pl.BlockSpec(memory_space=pltpu.VMEM) if full is None else ANY)] * outs,
        [
            pltpu.VMEM((2, 3, depth, height * breadth), jnp.bfloat16),
            pltpu.VMEM((2, height + 2, breadth, total), jnp.bfloat16),
            pltpu.VMEM((3, 3 * depth, total), jnp.float32),
            pltpu.VMEM((3, 3 * depth, total if arrived else LANES), jnp.bfloat16),
            pltpu.SemaphoreType.DMA((2, waits)),
            pltpu.SemaphoreType.DMA((waits, count)),
            pltpu.SemaphoreType.DMA((2, count, 2)),
            pltpu.SemaphoreType.DMA((count, parts)),
            pltpu.SemaphoreType.DMA((count,)),
            pltpu.SemaphoreType.DMA((count,)),
        ],
        (4 * 9 * depth * total * height * breadth, moved),
    )


def add_blocks(places, arrived, out, after):
    taps, depth, width = arrived[0].shape
    count = len(arrived)

    def body(*refs):
        arrived_refs = refs[:count]
        out_ref, came, held, sems = refs[-4:]
        steps = [(b, k) for b in range(count) for k in range(taps)]
        columns = [column_slice(place(), width) for place in places]

        def there(b, k):
            return out_ref.at[k, :, columns[b]]

        loads = [
            (
                pltpu.make_async_copy(arrived_refs[b].at[k], came.at[b, k], sems.at[0, b, k]),
                pltpu.make_async_copy(there(b, k), held.at[b, k], sems.at[1, b, k]),
            )
            for b, k in steps
        ]
        stores = [
            pltpu.make_async_copy(held.at[b, k], there(b, k), sems.at[2, b, k]) for b, k in steps
        ]
        for pair in loads:
            for c in pair:
                c.start()
        for n, (b, k) in enumerate(steps):
            for c in loads[n]:
                c.wait()
            held[b, k] += came[b, k].astype(jnp.float32)
            stores[n].start()
        for c in stores:
            c.wait()

    return pl.pallas_call(
        body,
        in_specs=[ANY] * (count + 1 + len(after)),
        out_specs=ANY,
        scratch_shapes=[
            pltpu.VMEM((count, taps, depth, width), jnp.bfloat16),
            pltpu.VMEM((count, taps, depth, width), jnp.float32),
            pltpu.SemaphoreType.DMA((3, count, taps)),
        ],
        out_shape=jax.ShapeDtypeStruct(out.shape, jnp.float32),
        input_output_aliases={count: 0},
        compiler_params=params(),
        cost_estimate=cost(count * taps * depth * width, 10 * count * taps * depth * width),
        name="add_blocks",
    )(*arrived, out, *after)


def cut_share(grad, block, share, width, after):
    breadth = grad.shape[1]

    def body(grad_ref, *refs):
        out_ref, sem = refs[-2:]
        chan = lax.axis_index("chan")
        load = pltpu.make_async_copy(
            grad_ref.at[
                pl.ds(chan % 2 * share, share), :, column_slice(chan // 2 * 2 + block, width)
            ],
            out_ref,
            sem,
        )
        load.start()
        load.wait()

    return pl.pallas_call(
        body,
        in_specs=[ANY] * (1 + len(after)),
        out_specs=pl.BlockSpec(memory_space=pltpu.VMEM),
        scratch_shapes=[pltpu.SemaphoreType.DMA],
        out_shape=jax.ShapeDtypeStruct((share, breadth, width), grad.dtype),
        compiler_params=params(),
        cost_estimate=cost(0, 4 * share * breadth * width),
        name="cut_share",
    )(grad, *after)


def block_part(grad, rims, weights, tops, unit):
    height, breadth, filters = grad.shape
    depth = weights.shape[1] // 3
    span, count = unit * breadth, len(tops)
    lane = min(depth, LANES)

    def body(inputs, out_refs, scratch):
        grad_any, rims_any, weights_any = inputs
        (out_ref,) = out_refs
        grads, taps, sums, results, g_sem, r_sem, w_sem, o_sem = scratch

        def rows_of(n):
            top = tops[n]
            low, high = max(top - 1, 0), min(top + unit + 1, height)
            copies = [
                pltpu.make_async_copy(
                    grad_any.at[pl.ds(low, high - low)],
                    grads.at[n, pl.ds(low - top + 1, high - low)],
                    g_sem.at[n],
                )
            ]
            for e, edge in enumerate((low == top, high == top + unit)):
                if edge:
                    copies.append(
                        pltpu.make_async_copy(
                            rims_any.at[pl.ds(e, 1)],
                            grads.at[n, pl.ds(e * (unit + 1), 1)],
                            r_sem.at[n, e],
                        )
                    )
            return copies

        loads = [
            pltpu.make_async_copy(
                weights_any.at[r, pl.ds(s * depth, depth)],
                taps.at[r, pl.ds(s * depth, depth)],
                w_sem.at[r, s],
            )
            for r in range(3)
            for s in range(3)
        ]
        groups = [rows_of(0) + loads[:1], loads[1:3], loads[3:6], loads[6:]]
        groups += [rows_of(n) for n in range(1, count)]
        stream = Stream(groups, 2)
        yield
        waits = {0: 0, 1: 1, 3: 2, 6: 3}
        column = lax.broadcasted_iota(jnp.int32, (unit, breadth, lane), 1).reshape(span, lane)
        stores = []
        for n, top in enumerate(tops):
            if n > 0:
                stream.wait(3 + n)
            for r in range(3):
                for s in range(3):
                    if n == 0 and 3 * r + s in waits:
                        stream.wait(waits[3 * r + s])
                    moved = grads[n, 2 - r : 2 - r + unit].reshape(span, filters)
                    product = lax.dot_general(
                        moved,
                        taps[r, s * depth : (s + 1) * depth, :],
                        (((1,), (1,)), ((), ())),
                        preferred_element_type=jnp.float32,
                    )
                    if r == 0:
                        sums[s] = product
                    else:
                        sums[s] += product
            for low in range(0, depth, lane):
                before = pltpu.roll(sums[2, :, low : low + lane], 1, 0)
                behind = pltpu.roll(sums[0, :, low : low + lane], span - 1, 0)
                value = (
                    sums[1, :, low : low + lane]
                    + jnp.where(column == 0, 0.0, before)
                    + jnp.where(column == breadth - 1, 0.0, behind)
                )
                results[n, :, :, low : low + lane] = value.astype(jnp.bfloat16).reshape(
                    unit, breadth, lane
                )
            stores.append(
                pltpu.make_async_copy(results.at[n], out_ref.at[pl.ds(n * unit, unit)], o_sem.at[n])
            )
            stores[-1].start()
        for c in stores:
            c.wait()

    shape = jax.ShapeDtypeStruct((count * unit, breadth, depth), jnp.bfloat16)
    return Part(
        body,
        [grad, rims, weights],
        [(shape, ANY)],
        [
            pltpu.VMEM((count, unit + 2, breadth, filters), jnp.bfloat16),
            pltpu.VMEM(weights.shape, jnp.bfloat16),
            pltpu.VMEM((3, span, depth), jnp.float32),
            pltpu.VMEM((count, unit, breadth, depth), jnp.bfloat16),
            pltpu.SemaphoreType.DMA((count,)),
            pltpu.SemaphoreType.DMA((count, 2)),
            pltpu.SemaphoreType.DMA((3, 3)),
            pltpu.SemaphoreType.DMA((count,)),
        ],
        (18 * count * unit * breadth * depth * filters, 2 * weights.size),
    )


def per_device(saved_input, upstream, kernel):
    height, breadth, filters = upstream.shape
    part = saved_input.shape[1]
    channels = kernel.shape[2]
    tiles, chans, filts = (lax.axis_size(a) for a in ("tile", "chan", "filt"))
    tile, filt = (lax.axis_index(a) for a in ("tile", "filt"))
    depth = channels // tiles

    def chunk(bits, saved=saved_input):
        return lax.dynamic_slice_in_dim(saved, (tile ^ bits) * depth, depth, axis=2)

    def columns(value):
        if filts == 2:
            return [value, swap(value, "filt", 1)]
        return [lax.all_gather(value, "filt", axis=1, tiled=True)]

    sent_far = chunk(2)
    pair_far = swap(sent_far, "tile", 1)
    own_far = columns(chunk(3))

    even = tile % 2 == 0
    first, last = upstream[:1], upstream[height - 1 :]
    up = [(i, i + 1) for i in range(tiles - 1)]
    inward, outward = jnp.where(even, last, first), jnp.where(even, first, last)
    above = lax.ppermute(last, "tile", up)
    below = lax.ppermute(first, "tile", [(j, i) for i, j in up])
    across = lax.ppermute(outward, "tile", [(1, 3), (2, 0)])
    rims = jnp.concatenate(
        [above, below, jnp.where(even, inward, across), jnp.where(even, across, inward)], axis=0
    )

    weights = kernel.reshape(3, 3 * channels, filters)
    unit = largest(height, 16)
    tops = list(range(0, height, unit))
    halves = [h for h in (tops[:1], tops[1:]) if h]
    partials = []

    def next_rows(after):
        part_ = block_part(upstream, rims, weights, halves[len(partials)], unit)
        ((partial,),) = run("block_grad", [part_], after)
        partials.append(partial)
        return [partial]

    if chans == 4 and filters % (4 * LANES) == 0 and height % 2 == 0:
        share, width = height // 2, filters // 4
        near_cut = cut_share(upstream, 0, share, width, [pair_far, *own_far])
        far_cut = cut_share(upstream, 1, share, width, [near_cut, rims])
        own_far = shifted_active(own_far, [far_cut])
        fetched = [swap(near_cut, "tile", 1), swap(far_cut, "tile", 1)]
        pair_far = shifted_active(columns(pair_far), [own_far])
        fetched[0], _ = lax.optimization_barrier((fetched[0], pair_far))
        crossed = [swap(v, "chan", 2) for v in fetched]
        pieces = [[v, swap(v, "chan", 1)] for v in fetched]

        def place_of(j):
            return lambda: (lax.axis_index("chan") // 2 ^ (j // 2)) * 2 + j % 2

        def order(k):
            return lax.axis_index("chan") % 2 ^ k

        groups = [[0], [1], [2, 3]]
    else:
        own_far = shifted_active(own_far, [])
        pair_far = shifted_active(columns(pair_far), [own_far])
        crossed, pieces = [], [[swap(upstream, "tile", 1)]]

        def place_of(j):
            return lambda: 0

        def order(k):
            return 0

        groups = [[0]]
    chain = [pair_far]
    arrived = []
    saved, _ = lax.optimization_barrier((saved_input, pair_far))
    pair_near = swap(chunk(1, saved), "tile", 1)
    for n, group in enumerate(groups):
        if n == 2:
            pieces += [[v, swap(v, "chan", 1)] for v in crossed]
        blocks = [(place_of(j), v) for j, v in enumerate(pieces)]
        sums = sums_part(
            [blocks[j] for j in group], order, (own_far, 0), (pair_far, 0), upstream, rims
        )
        (far,) = run("kernel_sums", [sums], chain)
        chain = [far[-1]]
        arrived += [swap(v, "tile", 3) for v in far]
        if n == 0:
            pair_near, _ = lax.optimization_barrier((pair_near, far[0]))
            near = columns(jnp.concatenate([chunk(0), pair_near], axis=0))
            chain = next_rows(chain)
    while len(partials) < len(halves):
        chain = next_rows(chain)
    near = shifted_active(near, chain)
    early = len(arrived) // 2
    last = sums_part(blocks, order, (near, 0), (near, 1), upstream, rims, arrived[:early], filters)
    ((out,),) = run("kernel_sums", [last], [near])
    summed = []
    for partial in partials:
        if filts == 2:
            mine = lax.dynamic_slice_in_dim(partial, filt * part, part, axis=1)
            other = lax.dynamic_slice_in_dim(partial, (1 - filt) * part, part, axis=1)
            total = mine.astype(jnp.float32) + swap(other, "filt", 1).astype(jnp.float32)
        else:
            total = lax.psum_scatter(partial, "filt", scatter_dimension=1, tiled=True).astype(
                jnp.float32
            )
        summed.append(total)
    masked = jnp.where(saved_input > 0, jnp.concatenate(summed, 0), jnp.zeros((), jnp.float32))
    input_grad = masked.astype(jnp.bfloat16)
    places = [place for place, _ in blocks[early:]]
    out = add_blocks(places, arrived[early:], out, [input_grad])
    return input_grad, out.reshape(3, 3, depth, filters)


def solution(mesh):
    placed = (P("tile", "filt", "chan"), P("tile", None, "filt"), P(None, None, "chan", "filt"))
    return jax.shard_map(
        per_device,
        mesh=mesh,
        in_specs=placed,
        out_specs=(P("tile", "filt", "chan"), P(None, None, ("chan", "tile"), "filt")),
        check_vma=False,
    )
```
